512 devices in a mesh: member: 32 (over x, z), patch: 16 (over y, core).
Axes of the slice: x: 4, y: 8, z: 8, core: 2. Of those that a mesh axis runs over, the one named last changes fastest.
Arguments:
- background_fields: bfloat16 [512, 960, 384], P('patch', 'member')
- measured_location: int32 [512, 640], P('patch'), may hold values from 0 to 767
- measured_datum: float32 [512, 640], P('patch'), may hold values from -6 to 6
- measured_error_spread: float32 [512, 640], P('patch'), may hold values from 0.3 to 3
- measured_distance_band: int32 [512, 640], P('patch'), may hold values from 0 to 15
- measured_tally: int32 [512], P('patch'), may hold values from 160 to 640, as said below
- taper_weights: int32 [16], replicated, may hold values from 8 to 64
Outputs:
- analysis: bfloat16 [512, 960, 384], P('patch', 'member')
The draws below stay inside these ranges and needn't reach their ends.
Inputs may be any that keep to these rules, and one draw needn't show every extreme that they name: `measured_tally`: the live observations of a patch fill its first slots; at least one patch fills all 640.
All inputs are finite; a program needn't handle non-finite values.
Results may differ from the reference program's by a relative error of at most 0.006.
Values may be sent and summed in bfloat16 or wider, within the bound.
No kernel may reach another device: no remote copies, remote signals or barrier semaphores. Data moves between devices by JAX's collectives and lax.ppermute only.
A program may use at most 64 MiB of HBM per device.

```python
import math
import jax
import jax.numpy as jnp
from jax import lax

MEMBERS = 960
STRATUM_PAIRS = 24
PIECE_WIDTH = 16
FRINGE_REACH = 8
SPAN_WIDTH = 32
OBS = 640
NCLASS = 16
PATCHES = 512


def draw_background_fields(key, part):
    key = jax.random.fold_in(key, 11)
    base_key, spread_key, noise_key = jax.random.split(key, 3)
    full_shape = (PATCHES, MEMBERS, STRATUM_PAIRS * PIECE_WIDTH)
    background = jax.random.normal(base_key, (PATCHES, 1, STRATUM_PAIRS * PIECE_WIDTH), jnp.float32)
    spread = jnp.exp(jax.random.uniform(spread_key, (PATCHES, 1, STRATUM_PAIRS * PIECE_WIDTH), jnp.float32, math.log(0.4), math.log(1.6)))
    member_noise = jax.random.normal(noise_key, full_shape, jnp.float32)
    return (background + spread * member_noise).astype(jnp.bfloat16)


def draw_measured_tally(key, part):
    key = jax.random.fold_in(key, 23)
    count_key, pick_key = jax.random.split(key)
    counts = jax.random.randint(count_key, (PATCHES,), OBS // 4, OBS + 1)
    fullest = jax.random.randint(pick_key, (), 0, PATCHES)
    return counts.at[fullest].set(OBS).astype(jnp.int32)


def plant(array, own_key, least, largest):
    longest = array.shape.index(max(array.shape))
    spots = []
    for shift in (0, 1):
        where = [jax.random.randint(jax.random.fold_in(own_key, axis), (), 0, length) for axis, length in enumerate(array.shape)]
        where[longest] = (where[longest] + shift) % array.shape[longest]
        spots.append(tuple(where))
    return array.at[spots[0]].set(least).at[spots[1]].set(largest)


def shard_levels(own_key, dims, pieces, smallest, top_value):
    factor_of, own = 1.0, jax.random.fold_in(own_key, 6)
    for axis_at, parts in pieces:
        heights = jnp.exp(jax.random.uniform(jax.random.fold_in(own, axis_at), (parts,), jnp.float32, smallest / len(pieces), top_value / len(pieces)))
        factor_of = factor_of * jnp.repeat(heights, dims[axis_at] // parts).reshape([-1 if axis == axis_at else 1 for axis in range(len(dims))])
    return factor_of


def gaussian(rng, shape, width, limit, pieces=(), held_as=jnp.bfloat16):
    loudness = shard_levels(rng, shape, pieces, -0.22, 0.18) if pieces else 1.0
    values = jax.random.normal(rng, shape, jnp.float32) * width * loudness
    return jnp.minimum(jnp.maximum(values, -limit), limit).astype(held_as)


def setup_inputs(seed: int = 0) -> dict:
    key_list = jax.random.split(jax.random.key(seed), 8)
    return {
        "background_fields": draw_background_fields(jax.random.fold_in(key_list[7], 71), 0),
        "measured_location": plant(jax.random.randint(key_list[1], (PATCHES, OBS), 0, STRATUM_PAIRS * SPAN_WIDTH), jax.random.fold_in(key_list[1], 1), 0, (STRATUM_PAIRS * SPAN_WIDTH) - 1).astype(jnp.int32),
        "measured_datum": gaussian(key_list[2], (PATCHES, OBS), 1.0, 6.0, ((0, 16),), jnp.float32),
        "measured_error_spread": jnp.clip(jnp.exp(math.log(3.0) - 2.3025851 * jax.random.uniform(key_list[3], (PATCHES, OBS), jnp.float32) ** shard_levels(key_list[3], (PATCHES, OBS), ((0, 16),), -0.2, 0.2)), 0.3, 3.0),
        "measured_distance_band": plant(jax.random.randint(key_list[4], (PATCHES, OBS), 0, NCLASS), jax.random.fold_in(key_list[4], 1), 0, NCLASS - 1).astype(jnp.int32),
        "measured_tally": draw_measured_tally(jax.random.fold_in(key_list[7], 71), 0),
        "taper_weights": plant(jax.random.randint(key_list[6], (NCLASS,), 8, 65), jax.random.fold_in(key_list[6], 1), 8, 64).astype(jnp.int32),
    }


def patch_weights(sensed_reading, values, variance, classes, obs_total, taper_weights):
    trial_predictions = sensed_reading.shape[0]
    obs_mean = lax.optimization_barrier(jnp.mean(sensed_reading.astype(jnp.float32), axis=0))
    slot_index = jnp.arange(sensed_reading.shape[1], dtype=jnp.int32)
    live_mask = (slot_index < obs_total).astype(jnp.float32)
    weight = taper_weights[classes].astype(jnp.float32) / 64.0
    precision = live_mask * weight / variance
    root_weight = jnp.sqrt(precision)
    scaled = (root_weight[None, :] * (sensed_reading.astype(jnp.float32) - obs_mean[None, :])).astype(jnp.bfloat16)
    innovation = (root_weight * (values - obs_mean)).astype(jnp.bfloat16)
    scaled_wide = scaled.astype(jnp.float32)
    gram_matrix = jnp.dot(scaled_wide, scaled_wide.T, precision=lax.Precision.HIGHEST)
    obs_pull = jnp.dot(scaled_wide, innovation.astype(jnp.float32), precision=lax.Precision.HIGHEST)
    draw_offset = jnp.float32(trial_predictions - 1)
    unit_matrix = jnp.eye(trial_predictions, dtype=jnp.float32)
    gram_trace = jnp.sum(jnp.diagonal(gram_matrix))
    norm_scale = draw_offset + 2.0 * jnp.sum(gram_matrix * gram_matrix) / (draw_offset + gram_trace)
    normal = (gram_matrix + draw_offset * unit_matrix) / norm_scale
    system = normal.astype(jnp.bfloat16)
    first_root = (1.5 * unit_matrix - 0.5 * normal).astype(jnp.bfloat16)
    first_wide = first_root.astype(jnp.float32)
    root_square = jnp.dot(first_wide, first_wide, precision=lax.Precision.HIGHEST).astype(jnp.bfloat16)
    product = jnp.dot(system.astype(jnp.float32), root_square.astype(jnp.float32), precision=lax.Precision.HIGHEST)
    correction = (1.5 * unit_matrix - 0.5 * product).astype(jnp.bfloat16)
    second_root = jnp.dot(first_wide, correction.astype(jnp.float32), precision=lax.Precision.HIGHEST)
    inner_step = jnp.dot(second_root, obs_pull, precision=lax.Precision.HIGHEST)
    mean_weights = jnp.dot(second_root, inner_step, precision=lax.Precision.HIGHEST) / norm_scale
    total_weights = jnp.sqrt(draw_offset / norm_scale) * second_root + mean_weights[:, None]
    return total_weights.astype(jnp.bfloat16)

def reference(background_fields, measured_location, measured_datum, measured_error_spread, measured_distance_band, measured_tally, taper_weights):
    tile_sequence = background_fields.shape[0]
    trial_predictions = background_fields.shape[1]

    def one_patch(tile_ordinal):
        former_piece_batch = lax.dynamic_index_in_dim(background_fields, (tile_ordinal + tile_sequence - 1) % tile_sequence, 0, keepdims=False)
        active_piece_batch = lax.dynamic_index_in_dim(background_fields, tile_ordinal, 0, keepdims=False)
        next_piece_batch = lax.dynamic_index_in_dim(background_fields, (tile_ordinal + 1) % tile_sequence, 0, keepdims=False)
        neighbour_span = jnp.concatenate([former_piece_batch.reshape(trial_predictions, STRATUM_PAIRS, PIECE_WIDTH)[:, :, PIECE_WIDTH - FRINGE_REACH:], active_piece_batch.reshape(trial_predictions, STRATUM_PAIRS, PIECE_WIDTH), next_piece_batch.reshape(trial_predictions, STRATUM_PAIRS, PIECE_WIDTH)[:, :, :FRINGE_REACH]], axis=2).reshape(trial_predictions, STRATUM_PAIRS * SPAN_WIDTH)
        positions = lax.dynamic_index_in_dim(measured_location, tile_ordinal, 0, keepdims=False)
        sensed_reading = jnp.take(neighbour_span, positions, axis=1)
        total_weights = patch_weights(sensed_reading, lax.dynamic_index_in_dim(measured_datum, tile_ordinal, 0, keepdims=False), lax.dynamic_index_in_dim(measured_error_spread, tile_ordinal, 0, keepdims=False), lax.dynamic_index_in_dim(measured_distance_band, tile_ordinal, 0, keepdims=False), lax.dynamic_index_in_dim(measured_tally, tile_ordinal, 0, keepdims=False), taper_weights)
        state_mean = lax.optimization_barrier(jnp.mean(active_piece_batch.astype(jnp.float32), axis=0))
        spread = (active_piece_batch.astype(jnp.float32) - state_mean[None, :]).astype(jnp.bfloat16)
        moved = jnp.dot(total_weights.astype(jnp.float32).T, spread.astype(jnp.float32), precision=lax.Precision.HIGHEST)
        return (state_mean[None, :] + moved).astype(jnp.bfloat16)
    return lax.map(one_patch, jnp.arange(tile_sequence, dtype=jnp.int32))
```

```python
import jax
import jax.numpy as jnp
from jax import lax
from jax.experimental import pallas as pl
from jax.experimental.pallas import tpu as pltpu
from jax.sharding import PartitionSpec as P

STRATUM_PAIRS = 24
PIECE_WIDTH = 16
FRINGE_REACH = 8
SPAN_WIDTH = 32
NCLASS = 16
CORE = STRATUM_PAIRS * PIECE_WIDTH
RIM = STRATUM_PAIRS * FRINGE_REACH
OBS = 640
HELD = 30
PADDED = 32
TILE = 256

F32 = jnp.float32
BF16 = jnp.bfloat16
I32 = jnp.int32


def vmem():
    return pl.BlockSpec(memory_space=pltpu.VMEM)


def smem():
    return pl.BlockSpec(memory_space=pltpu.SMEM)


def params():
    return pltpu.CompilerParams(vmem_limit_bytes=40 * 1024 * 1024)


def mm(a, b):
    return jnp.dot(a, b, preferred_element_type=F32)


def one_hot(rows, wanted):
    row = lax.broadcasted_iota(I32, (rows, wanted.shape[1]), 0)
    return jnp.where(row == wanted, 1.0, 0.0).astype(BF16)


def prep_kernel(
    me, tally, taper, location, datum, error_spread, band,
    pick_core, pick_even, pick_odd, pack_even, pack_odd, slots,
):
    mine = pl.ds(me[0], 1)
    flat = location[mine, :]
    level = flat >> 5
    column = flat & 31
    in_core = (column >= FRINGE_REACH) & (column < FRINGE_REACH + PIECE_WIDTH)
    core_index = jnp.where(in_core, level * PIECE_WIDTH + column - FRINGE_REACH, -1)
    pick_core[...] = one_hot(CORE, core_index)
    rim_index = level * FRINGE_REACH + (column & 7)
    side = jnp.where(column < FRINGE_REACH, 0, TILE)
    even_index = jnp.where(in_core, -1, rim_index + side)
    odd_index = jnp.where(rim_index < 128, even_index, even_index + 64)
    odd_index = jnp.where(in_core, -1, odd_index)
    pick_even[...] = one_hot(2 * TILE, even_index)
    pick_odd[...] = one_hot(2 * TILE, odd_index)

    lane = lax.broadcasted_iota(I32, (1, 2 * CORE), 1)
    leftward = lane >= CORE
    lane = jnp.where(leftward, lane - CORE, lane)
    shift = jnp.where(leftward, 0, PIECE_WIDTH - FRINGE_REACH)
    rim_even = jnp.where(lane < 128, lane, jnp.where((lane >= 256) & (lane < 320), lane - 128, -1))
    rim_odd = jnp.where((lane >= 128) & (lane < 256), lane - 128, jnp.where(lane >= 320, lane - 192, -1))
    for rim, out in ((rim_even, pack_even), (rim_odd, pack_odd)):
        source = (rim >> 3) * PIECE_WIDTH + (rim & 7) + shift
        out[...] = one_hot(CORE, jnp.where(rim >= 0, source, -1))

    classes = band[mine, :]
    weight = jnp.zeros(classes.shape, I32)
    for k in range(NCLASS):
        weight = jnp.where(classes == k, taper[k], weight)
    slot = lax.broadcasted_iota(I32, classes.shape, 1)
    live = jnp.where(slot < tally[me[0]], 1.0, 0.0)
    precision = live * (weight.astype(F32) / 64.0) / error_spread[mine, :]
    slots[0:1, :] = jnp.sqrt(precision)
    slots[1:2, :] = datum[mine, :]


def rims_kernel(received, pack_even, pack_odd, states, rightward, leftward):
    sources = received.shape[0]
    half = states.shape[0] // 2
    states[...] = jnp.zeros(states.shape, states.dtype)
    for j in range(sources):
        start = (j % 2) * half + (j // 2) * PADDED
        states[start : start + HELD, :] = received[j]
    for t in range(0, half, TILE):
        rims = mm(states[t : t + TILE, :], pack_even[...])
        rims += mm(states[half + t : half + t + TILE, :], pack_odd[...])
        rims = rims.astype(BF16)
        rightward[t : t + TILE, :] = rims[:, :CORE]
        leftward[t : t + TILE, :] = rims[:, CORE:]


def row_live(rows, columns):
    return (lax.broadcasted_iota(I32, (rows, columns), 0) & (PADDED - 1)) < HELD


def core_kernel(members, states, pick_core, partial, spread, state_mean):
    rows = states.shape[0]
    total = jnp.zeros((1, CORE), F32)
    for t in range(0, rows, TILE):
        total += jnp.sum(states[t : t + TILE, :].astype(F32), axis=0, keepdims=True)
    mean = total / members
    state_mean[0:1, :] = mean
    live = row_live(TILE, CORE)
    for t in range(0, rows, TILE):
        tile = states[t : t + TILE, :]
        partial[t : t + TILE, :] = mm(tile, pick_core[...]).astype(BF16)
        spread[t : t + TILE, :] = jnp.where(live, tile.astype(F32) - mean, 0.0).astype(BF16)


def main_kernel(
    members, partial, spread, state_mean, before, after, pick_even, pick_odd, slots,
    out, observed, scaled, scaled_t, gram, gram_n, basis, chain,
):
    rows = partial.shape[0]
    half = rows // 2
    draw = F32(members - 1)
    total = jnp.zeros((1, OBS), F32)
    for t in range(0, rows, TILE):
        odd = t >= half
        pick = pick_odd if odd else pick_even
        place = slice(t % half, t % half + TILE)
        tile = partial[t : t + TILE, :].astype(F32)
        for rims, top in ((before, 0), (after, TILE)):
            if odd:
                tile += mm(rims[place, 128:384], pick[top : top + TILE, :])
            else:
                tile += mm(rims[place, 0:128], pick[top : top + 128, :])
                tile += mm(rims[place, 256:384], pick[top + 128 : top + TILE, :])
        total += jnp.sum(tile, axis=0, keepdims=True)
        observed[t : t + TILE, :] = tile.astype(BF16)
    obs_mean = total / members
    root = slots[0:1, :]
    innovation = (root * (slots[1:2, :] - obs_mean)).astype(BF16).astype(F32)
    live = row_live(TILE, OBS)
    for t in range(0, rows, TILE):
        tile = root * (observed[t : t + TILE, :].astype(F32) - obs_mean)
        tile = jnp.where(live, tile, 0.0)
        scaled[t : t + TILE, :] = tile.astype(BF16)
        scaled_t[:, t : t + TILE] = tile.T.astype(BF16)
    pulls = jnp.broadcast_to(innovation, (128, OBS)).T

    squares = jnp.zeros((1, 1), F32)
    trace = jnp.zeros((1, 1), F32)
    corner = lax.broadcasted_iota(I32, (128, 128), 0) == lax.broadcasted_iota(I32, (128, 128), 1)
    for t in range(0, OBS, 128):
        block = mm(scaled_t[t : t + 128, :], scaled[...])
        gram[t : t + 128, :] = block
        squares += jnp.sum(block * block, keepdims=True)
        trace += jnp.sum(jnp.where(corner, block[:, t : t + 128], 0.0), keepdims=True)
    norm_scale = draw + 2.0 * squares / (draw + trace)
    inverse = 1.0 / norm_scale
    gram_n[...] = (gram[...] * inverse).astype(BF16)
    basis[...] = mm(scaled_t[...], spread[...]) * inverse

    a = draw * inverse
    r = 1.5 - 0.5 * a
    z = basis[...]
    v = -0.5 * z
    d = pulls
    product = mm(gram_n[...], jnp.concatenate([v, d], axis=1).astype(BF16))
    v = 2.0 * r * v - 0.5 * product[:, :CORE]
    x = r * d - 0.5 * product[:, CORE:]
    product = mm(gram_n[...], jnp.concatenate([v, x], axis=1).astype(BF16))
    v = -0.5 * (r * r * z + a * v + product[:, :CORE])
    x = r * x - 0.5 * product[:, CORE:]
    product = mm(gram_n[...], jnp.concatenate([v, x], axis=1).astype(BF16))
    s = 1.5 - 0.5 * a * r * r
    v = r * v - 0.5 * s * z - 0.5 * product[:, :CORE]
    chain[...] = v
    x = 1.5 * d - 0.5 * (a * x + product[:, CORE:])
    x = r * x - 0.5 * mm(gram_n[...], x.astype(BF16))
    y = mm(gram_n[...], x.astype(BF16))
    shift = []
    for t in range(0, CORE, 128):
        both = r * s * x * z[:, t : t + 128] + y * v[:, t : t + 128]
        shift.append(jnp.sum(both, axis=0, keepdims=True))
    base = state_mean[0:1, :] + jnp.concatenate(shift, axis=1)
    lift = chain[...].astype(BF16)
    gain = jnp.sqrt(a)
    for t in range(0, rows, TILE):
        moved = mm(scaled[t : t + TILE, :], lift) + r * s * spread[t : t + TILE, :].astype(F32)
        result = (base + gain * moved).astype(BF16)
        for u in range(0, TILE, PADDED):
            j = 2 * ((t % half + u) // PADDED) + t // half
            out[j] = result[u : u + HELD, :]


def shape(*dims, dtype=BF16):
    return jax.ShapeDtypeStruct(dims, dtype)


def prepare(me, measured_tally, taper_weights, location, datum, error_spread, band):
    return pl.pallas_call(
        prep_kernel,
        in_specs=[smem()] * 3 + [vmem()] * 4,
        out_specs=[vmem()] * 6,
        out_shape=[
            shape(CORE, OBS), shape(2 * TILE, OBS), shape(2 * TILE, OBS),
            shape(CORE, 2 * CORE), shape(CORE, 2 * CORE), shape(8, OBS, dtype=F32),
        ],
        compiler_params=params(),
        name="prepare",
    )(me, measured_tally, taper_weights, location, datum, error_spread, band)


def extract(received, pack_even, pack_odd):
    rows = received.shape[0] * PADDED
    return pl.pallas_call(
        rims_kernel,
        in_specs=[vmem()] * 3,
        out_specs=[vmem()] * 3,
        out_shape=[shape(rows, CORE), shape(rows // 2, CORE), shape(rows // 2, CORE)],
        compiler_params=params(),
        name="extract",
    )(received, pack_even, pack_odd)


def core_part(members, states, pick_core):
    rows = states.shape[0]
    return pl.pallas_call(
        lambda *refs: core_kernel(members, *refs),
        in_specs=[vmem()] * 2,
        out_specs=[vmem()] * 3,
        out_shape=[shape(rows, OBS), shape(rows, CORE), shape(8, CORE, dtype=F32)],
        compiler_params=params(),
        cost_estimate=pl.CostEstimate(
            flops=2 * rows * CORE * OBS, bytes_accessed=4 * rows * OBS, transcendentals=0
        ),
        name="core_part",
    )(states, pick_core)


def analyse(members, partial, spread, state_mean, before, after, pick_even, pick_odd, slots):
    rows = partial.shape[0]
    return pl.pallas_call(
        lambda *refs: main_kernel(members, *refs),
        in_specs=[vmem()] * 8,
        out_specs=vmem(),
        out_shape=shape(rows // PADDED, HELD, CORE),
        scratch_shapes=[
            pltpu.VMEM((rows, OBS), BF16),
            pltpu.VMEM((rows, OBS), BF16),
            pltpu.VMEM((OBS, rows), BF16),
            pltpu.VMEM((OBS, OBS), F32),
            pltpu.VMEM((OBS, OBS), BF16),
            pltpu.VMEM((OBS, CORE), F32),
            pltpu.VMEM((OBS, CORE), F32),
        ],
        compiler_params=params(),
        cost_estimate=pl.CostEstimate(
            flops=2 * rows * OBS * 3 * OBS, bytes_accessed=8 * rows * OBS, transcendentals=0
        ),
        name="analyse",
    )(partial, spread, state_mean, before, after, pick_even, pick_odd, slots)


def local(
    background_fields,
    measured_location,
    measured_datum,
    measured_error_spread,
    measured_distance_band,
    measured_tally,
    taper_weights,
):
    axes = ("member", "patch")
    groups, group = lax.axis_size("patch"), lax.axis_size("member")
    members = background_fields.shape[1] * group
    owners = [(g % group) * groups + g // group for g in range(group * groups)]
    me = lax.axis_index("member").astype(I32).reshape(1)
    received = lax.all_to_all(background_fields, "member", split_axis=0, concat_axis=0, tiled=True)
    pick_core, pick_even, pick_odd, pack_even, pack_odd, slots = prepare(
        me, measured_tally, taper_weights, measured_location, measured_datum,
        measured_error_spread, measured_distance_band,
    )
    states, rightward, leftward = extract(received, pack_even, pack_odd)
    up = list(zip(owners, owners[1:] + owners[:1]))
    down = [(j, i) for i, j in up]
    before = lax.ppermute(rightward, axes, up)
    after = lax.ppermute(leftward, axes, down)
    partial, spread, state_mean = core_part(members, states, pick_core)
    analysed = analyse(
        members, partial, spread, state_mean, before, after, pick_even, pick_odd, slots
    )
    return lax.all_to_all(analysed, "member", split_axis=0, concat_axis=0, tiled=True)


def solution(mesh):
    placed = (
        P("patch", "member", None),
        P("patch", None),
        P("patch", None),
        P("patch", None),
        P("patch", None),
        P("patch"),
        P(),
    )
    return jax.shard_map(
        local, mesh=mesh, in_specs=placed, out_specs=P("patch", "member", None), check_vma=False
    )
```

```python
import jax
import jax.numpy as jnp
import numpy as np
from jax import lax
from jax.experimental import pallas as pl
from jax.experimental.pallas import tpu as pltpu
from jax.sharding import PartitionSpec as P

STRATUM_PAIRS = 24
PIECE_WIDTH = 16
FRINGE_REACH = 8
NCLASS = 16
CORE = STRATUM_PAIRS * PIECE_WIDTH
RIM = STRATUM_PAIRS * FRINGE_REACH
SPAN = CORE + 2 * RIM
OBS = 640
GROUP = 32
HELD = 30
PADDED = 32
ROWS = GROUP * PADDED
MEMBERS = GROUP * HELD
HALF = 16
TILE = 256

F32 = jnp.float32
BF16 = jnp.bfloat16
I32 = jnp.int32

CYCLES = (
    (0, 8, 9, 17, 16, 23, 22, 14, 15, 7, 6, 5, 13, 21, 20, 12,
     4, 3, 2, 1, 25, 26, 18, 10, 11, 19, 27, 28, 29, 30, 31, 24),
    (0, 1, 9, 10, 2, 26, 27, 3, 11, 12, 13, 14, 6, 30, 22, 21,
     29, 5, 4, 28, 20, 19, 18, 17, 25, 24, 16, 8, 15, 23, 31, 7),
)
HOMES = np.array(CYCLES, np.int32).reshape(-1)
HOSTED = np.argsort(np.array(CYCLES, np.int32), axis=1).astype(np.int32).reshape(-1)


def vmem():
    return pl.BlockSpec(memory_space=pltpu.VMEM)


def smem():
    return pl.BlockSpec(memory_space=pltpu.SMEM)


def params():
    return pltpu.CompilerParams(vmem_limit_bytes=40 * 1024 * 1024)


def shape(*dims, dtype=BF16):
    return jax.ShapeDtypeStruct(dims, dtype)


def mm(a, b):
    return jnp.dot(a, b, preferred_element_type=F32)


def mm_nt(a, b):
    return lax.dot_general(a, b, (((1,), (1,)), ((), ())), preferred_element_type=F32)


def swap_matrix(rows, columns, inner):
    row = lax.broadcasted_iota(I32, (rows, columns), 0)
    column = lax.broadcasted_iota(I32, (rows, columns), 1)
    outer = rows // inner
    wanted = (row & (inner - 1)) * outer + row // inner
    return jnp.where(column == wanted, 1.0, 0.0).astype(BF16)


def entry_kernel(place, homes, states, out):
    first = place[0] * GROUP
    swap = swap_matrix(GROUP * HALF, GROUP * HALF, HALF)
    for start in (0, HALF):
        count = min(HALF, HELD - start)
        block = states[start : start + count].reshape(count * GROUP, CORE)
        moved = mm(swap[:, : count * GROUP], block).astype(BF16)
        for p in range(GROUP):
            out[homes[first + p], start : start + HALF, :] = moved[p * HALF : (p + 1) * HALF, :]


def exit_kernel(place, homes, analysed, out, ordered):
    first = place[0] * GROUP
    swap = swap_matrix(GROUP * HALF, GROUP * HALF, GROUP)
    for start in (0, HALF):
        count = min(HALF, HELD - start)
        for p in range(GROUP):
            ordered[p * HALF : (p + 1) * HALF, :] = analysed[homes[first + p], start : start + HALF, :]
        moved = mm(swap[: count * GROUP, :], ordered[...]).astype(BF16)
        out[start : start + count] = moved.reshape(count, GROUP, CORE)


def prepare_kernel(
    place, hosted, tally, taper, location, datum, error_spread, band,
    root_column, ratio_column, root_row, pick,
):
    me = hosted[place[0] * GROUP + place[1]]
    mine = pl.ds(me, 1)
    flat = location[mine, :]
    level = flat >> 5
    column = flat & 31
    spot = level * PIECE_WIDTH + column - FRINGE_REACH
    rim = level * FRINGE_REACH + (column & (FRINGE_REACH - 1))
    spot = jnp.where(column < FRINGE_REACH, CORE + rim, spot)
    spot = jnp.where(column >= FRINGE_REACH + PIECE_WIDTH, CORE + RIM + rim, spot)

    classes = band[mine, :]
    weight = jnp.zeros(classes.shape, I32)
    for k in range(NCLASS):
        weight = jnp.where(classes == k, taper[k], weight)
    slot = lax.broadcasted_iota(I32, classes.shape, 1)
    live = jnp.where(slot < tally[me], 1.0, 0.0)
    precision = live * (weight.astype(F32) / 64.0) / error_spread[mine, :]
    pulled = precision * datum[mine, :]
    for t in range(0, SPAN, 128):
        hit = lax.broadcasted_iota(I32, (128, OBS), 0) + t == spot
        total = jnp.sum(jnp.where(hit, precision, 0.0), axis=1, keepdims=True)
        pull = jnp.sum(jnp.where(hit, pulled, 0.0), axis=1, keepdims=True)
        total = jnp.broadcast_to(total, (128, 128))
        pull = jnp.broadcast_to(pull, (128, 128))
        root = jnp.sqrt(total)
        root_column[t : t + 128, :] = root
        ratio_column[t : t + 128, :] = jnp.where(
            total > 0.0, pull / jnp.where(total > 0.0, root, 1.0), 0.0
        )
        root_row[:, t : t + 128] = root.T[0:8, :]

    row = lax.broadcasted_iota(I32, (2 * RIM, CORE), 0)
    lane = lax.broadcasted_iota(I32, (2 * RIM, CORE), 1)
    rim = jnp.where(row < RIM, row, row - RIM)
    source = (rim >> 3) * PIECE_WIDTH + (rim & (FRINGE_REACH - 1))
    source = jnp.where(row < RIM, source + PIECE_WIDTH - FRINGE_REACH, source)
    pick[...] = jnp.where(lane == source, 1.0, 0.0).astype(BF16)


def extract_kernel(states, pick, rightward, leftward):
    for t in range(0, ROWS, TILE):
        rims = mm_nt(pick[...], states[t : t + TILE, :]).astype(BF16)
        rightward[:, t : t + TILE] = rims[:RIM, :]
        leftward[:, t : t + TILE] = rims[RIM:, :]


def own_kernel(
    states, root_column, ratio_column, root_row,
    spread, state_mean, gram, basis, pulls, sums,
):
    total = jnp.zeros((1, CORE), F32)
    for t in range(0, ROWS, TILE):
        total += jnp.sum(states[t : t + TILE, :].astype(F32), axis=0, keepdims=True)
    mean = total / MEMBERS
    state_mean[...] = jnp.broadcast_to(mean, (8, CORE))
    live = (lax.broadcasted_iota(I32, (TILE, CORE), 0) & (PADDED - 1)) < HELD
    covariance = jnp.zeros((CORE, CORE), F32)
    for t in range(0, ROWS, TILE):
        tile = jnp.where(live, states[t : t + TILE, :].astype(F32) - mean, 0.0)
        spread[t : t + TILE, :] = tile.astype(BF16)
        covariance += mm(tile.T.astype(BF16), tile.astype(BF16))
    squares = jnp.zeros((1, 1), F32)
    trace = jnp.zeros((1, 1), F32)
    corner = lax.broadcasted_iota(I32, (128, 128), 0) == lax.broadcasted_iota(I32, (128, 128), 1)
    column_mean = jnp.broadcast_to(mean, (128, CORE)).T
    for t in range(0, CORE, 128):
        root = root_column[t : t + 128, :]
        lifted = jnp.tile(root, (1, CORE // 128)) * covariance[t : t + 128, :]
        basis[t : t + 128, :] = lifted
        block = lifted * root_row[0:1, :CORE]
        gram[t : t + 128, :] = block.astype(BF16)
        squares += jnp.sum(block * block, keepdims=True)
        trace += jnp.sum(jnp.where(corner, block[:, t : t + 128], 0.0), keepdims=True)
        pulls[t : t + 128, :] = ratio_column[t : t + 128, :] - root * column_mean[t : t + 128, :]
    sums[0:8, :] = jnp.broadcast_to(squares, (8, 128))
    sums[8:16, :] = jnp.broadcast_to(trace, (8, 128))


def analyse_kernel(
    before, after, spread, state_mean, own_gram, own_basis, own_pulls, sums,
    root_column, ratio_column, root_row,
    out, fringe_t, fringe, gram, basis, pulls,
):
    live = (lax.broadcasted_iota(I32, (RIM, ROWS), 1) & (PADDED - 1)) < HELD
    for rims, top in ((before, 0), (after, RIM)):
        rows = slice(top, top + RIM)
        tile = rims[...].astype(F32)
        mean = jnp.sum(tile, axis=1, keepdims=True) / MEMBERS
        tile = jnp.where(live, tile - mean, 0.0)
        fringe_t[rows, :] = tile.astype(BF16)
        fringe[:, rows] = tile.T.astype(BF16)
        span = slice(CORE + top, CORE + top + RIM)
        pulls[span, :] = ratio_column[span, :] - root_column[span, :] * mean
    pulls[:CORE, :] = own_pulls[...]
    gram[:CORE, :CORE] = own_gram[...]
    basis[:CORE, :] = own_basis[...]

    squares = sums[0:1, 0:1]
    trace = sums[8:9, 0:1]
    corner = lax.broadcasted_iota(I32, (128, 128), 0) == lax.broadcasted_iota(I32, (128, 128), 1)
    for t in range(0, CORE, 128):
        root = root_column[CORE + t : CORE + t + 128, :]
        root = jnp.tile(root, (1, CORE // 128))
        lifted = root * mm(fringe_t[t : t + 128, :], spread[...])
        basis[CORE + t : CORE + t + 128, :] = lifted
        block = lifted * root_row[0:1, :CORE]
        gram[CORE + t : CORE + t + 128, :CORE] = block.astype(BF16)
        gram[:CORE, CORE + t : CORE + t + 128] = block.T.astype(BF16)
        squares += 2.0 * jnp.sum(block * block, keepdims=True)
        block = root * mm(fringe_t[t : t + 128, :], fringe[...]) * root_row[0:1, CORE:]
        gram[CORE + t : CORE + t + 128, CORE:] = block.astype(BF16)
        squares += jnp.sum(block * block, keepdims=True)
        trace += jnp.sum(jnp.where(corner, block[:, t : t + 128], 0.0), keepdims=True)
    draw = F32(MEMBERS - 1)
    inverse = 1.0 / (draw + 2.0 * squares / (draw + trace))

    a = draw * inverse
    r = 1.5 - 0.5 * a
    s = 1.5 - 0.5 * a * r * r
    z = basis[...] * inverse
    d = pulls[...]

    def step(*parts):
        both = jnp.concatenate(parts, axis=1).astype(BF16)
        product = mm(gram[...], both) * inverse
        return product[:, :CORE], product[:, CORE:]

    v = -0.5 * z
    pv, px = step(v, d)
    v = 2.0 * r * v - 0.5 * pv
    x = r * d - 0.5 * px
    pv, px = step(v, x)
    v = -0.5 * (r * r * z + a * v + pv)
    x = r * x - 0.5 * px
    pv, px = step(v, x)
    v = r * v - 0.5 * s * z - 0.5 * pv
    x = 1.5 * d - 0.5 * (a * x + px)
    x = r * x - 0.5 * inverse * mm(gram[...], x.astype(BF16))
    y = inverse * mm(gram[...], x.astype(BF16))
    shift = []
    for t in range(0, CORE, 128):
        both = r * s * x * z[:, t : t + 128] + y * v[:, t : t + 128]
        shift.append(jnp.sum(both, axis=0, keepdims=True))
    base = state_mean[0:1, :] + jnp.concatenate(shift, axis=1)
    lift = (jnp.tile(root_column[...], (1, CORE // 128)) * v).astype(BF16)
    gain = jnp.sqrt(a)
    for t in range(0, ROWS, TILE):
        own = spread[t : t + TILE, :]
        moved = mm(own, lift[:CORE, :]) + mm(fringe[t : t + TILE, :], lift[CORE:, :])
        moved += r * s * own.astype(F32)
        out[t : t + TILE, :] = (base + gain * moved).astype(BF16)


def call(kernel, name, smems, vmems, out_shape, scratch_shapes=(), flops=0):
    return pl.pallas_call(
        kernel,
        in_specs=[smem()] * smems + [vmem()] * vmems,
        out_specs=jax.tree.map(lambda _: vmem(), out_shape),
        out_shape=out_shape,
        scratch_shapes=list(scratch_shapes),
        compiler_params=params(),
        cost_estimate=pl.CostEstimate(flops=flops, bytes_accessed=1 << 20, transcendentals=0),
        name=name,
    )


def enter(place, homes, states):
    return call(
        entry_kernel, "entry", 2, 1, shape(GROUP, PADDED, CORE), flops=4 * 512 * 512 * CORE
    )(place, homes, states)


def leave(place, homes, analysed):
    return call(
        exit_kernel, "exit", 2, 1, shape(HELD, GROUP, CORE),
        [pltpu.VMEM((GROUP * HALF, CORE), BF16)], 4 * 512 * 512 * CORE,
    )(place, homes, analysed)


def prepare(place, hosted, tally, taper, location, datum, error_spread, band):
    return call(
        prepare_kernel, "prepare", 4, 4,
        [shape(SPAN, 128, dtype=F32), shape(SPAN, 128, dtype=F32), shape(8, SPAN, dtype=F32),
         shape(2 * RIM, CORE)],
        flops=4 * SPAN * OBS,
    )(place, hosted, tally, taper, location, datum, error_spread, band)


def extract(states, pick):
    return call(
        extract_kernel, "extract", 0, 2, [shape(RIM, ROWS), shape(RIM, ROWS)],
        flops=4 * RIM * CORE * ROWS,
    )(states, pick)


def own_part(states, root_column, ratio_column, root_row):
    return call(
        own_kernel, "own_part", 0, 4,
        [shape(ROWS, CORE), shape(8, CORE, dtype=F32), shape(CORE, CORE),
         shape(CORE, CORE, dtype=F32), shape(CORE, 128, dtype=F32), shape(16, 128, dtype=F32)],
        flops=2 * ROWS * CORE * CORE,
    )(states, root_column, ratio_column, root_row)


def analyse(before, after, own, prepared):
    return call(
        analyse_kernel, "analyse", 0, 11, shape(ROWS, CORE),
        [
            pltpu.VMEM((CORE, ROWS), BF16),
            pltpu.VMEM((ROWS, CORE), BF16),
            pltpu.VMEM((SPAN, SPAN), BF16),
            pltpu.VMEM((SPAN, CORE), F32),
            pltpu.VMEM((SPAN, 128), F32),
        ],
        8 * SPAN * SPAN * CORE,
    )(before, after, *own, *prepared)


def local(
    background_fields,
    measured_location,
    measured_datum,
    measured_error_spread,
    measured_distance_band,
    measured_tally,
    taper_weights,
):
    axes = ("member", "patch")
    groups = lax.axis_size("patch")
    place = jnp.stack([lax.axis_index("patch") % 2, lax.axis_index("member")]).astype(I32)
    homes = jnp.asarray(HOMES)
    sent = enter(place, homes, jnp.transpose(background_fields, (1, 0, 2)))
    received = lax.all_to_all(sent, "member", split_axis=0, concat_axis=0, tiled=True)
    *prepared, pick = prepare(
        place, jnp.asarray(HOSTED), measured_tally, taper_weights, measured_location,
        measured_datum, measured_error_spread, measured_distance_band,
    )
    states = received.reshape(ROWS, CORE)
    rightward, leftward = extract(states, pick)
    owners = [CYCLES[g % 2][p] * groups + g for g in range(groups) for p in range(GROUP)]
    up = list(zip(owners, owners[1:] + owners[:1]))
    down = [(j, i) for i, j in up]
    before = lax.ppermute(rightward, axes, up)
    after = lax.ppermute(leftward, axes, down)
    own = own_part(states, *prepared)
    analysed = analyse(before, after, own, prepared).reshape(GROUP, PADDED, CORE)
    returned = lax.all_to_all(analysed, "member", split_axis=0, concat_axis=0, tiled=True)
    return jnp.transpose(leave(place, homes, returned), (1, 0, 2))


def solution(mesh):
    placed = (
        P("patch", "member", None),
        P("patch", None),
        P("patch", None),
        P("patch", None),
        P("patch", None),
        P("patch"),
        P(),
    )
    return jax.shard_map(
        local, mesh=mesh, in_specs=placed, out_specs=P("patch", "member", None), check_vma=False
    )
```

```python
import jax
import jax.numpy as jnp
import numpy as np
from jax import lax
from jax.experimental import pallas as pl
from jax.experimental.pallas import tpu as pltpu
from jax.sharding import PartitionSpec as P

STRATUM_PAIRS = 24
PIECE_WIDTH = 16
FRINGE_REACH = 8
NCLASS = 16
CORE = STRATUM_PAIRS * PIECE_WIDTH
RIM = STRATUM_PAIRS * FRINGE_REACH
SPAN = CORE + 2 * RIM
OBS = 640
GROUP = 32
HELD = 30
PADDED = 32
ROWS = GROUP * PADDED
MEMBERS = GROUP * HELD
EIGHT = 8
TILE = 256

F32 = jnp.float32
BF16 = jnp.bfloat16
I32 = jnp.int32

CYCLES = (
    (0, 8, 9, 17, 16, 23, 22, 14, 15, 7, 6, 5, 13, 21, 20, 12,
     4, 3, 2, 1, 25, 26, 18, 10, 11, 19, 27, 28, 29, 30, 31, 24),
    (0, 1, 9, 10, 2, 26, 27, 3, 11, 12, 13, 14, 6, 30, 22, 21,
     29, 5, 4, 28, 20, 19, 18, 17, 25, 24, 16, 8, 15, 23, 31, 7),
)
HOSTED = np.argsort(np.array(CYCLES, np.int32), axis=1).astype(np.int32).reshape(-1)


def vmem():
    return pl.BlockSpec(memory_space=pltpu.VMEM)


def smem():
    return pl.BlockSpec(memory_space=pltpu.SMEM)


def hbm():
    return pl.BlockSpec(memory_space=pltpu.HBM)


def params():
    return pltpu.CompilerParams(vmem_limit_bytes=40 * 1024 * 1024)


def shape(*dims, dtype=BF16):
    return jax.ShapeDtypeStruct(dims, dtype)


def mm(a, b):
    return jnp.dot(a, b, preferred_element_type=F32)


def mm_nt(a, b):
    return lax.dot_general(a, b, (((1,), (1,)), ((), ())), preferred_element_type=F32)


def swap_matrix(inner):
    size = GROUP * EIGHT
    row = lax.broadcasted_iota(I32, (size, size), 0)
    column = lax.broadcasted_iota(I32, (size, size), 1)
    wanted = (row & (inner - 1)) * (size // inner) + row // inner
    return jnp.where(column == wanted, 1.0, 0.0).astype(BF16)


def core_index():
    return lax.axis_index("patch") % 2


def home_of(core, patch):
    return jnp.where(core == 0, CYCLES[0][patch], CYCLES[1][patch])


def entry_kernel(states, out):
    swap = swap_matrix(EIGHT)
    core = core_index()
    for start in range(0, HELD, 2 * EIGHT):
        halves = []
        for first in (start, start + EIGHT):
            count = min(EIGHT, HELD - first)
            block = states[first : first + count].reshape(count * GROUP, CORE)
            halves.append(mm(swap[:, : count * GROUP], block))
        for p in range(GROUP):
            rows = slice(p * EIGHT, (p + 1) * EIGHT)
            both = jnp.concatenate([half[rows, :] for half in halves], axis=0)
            out[home_of(core, p), start : start + 2 * EIGHT, :] = both.astype(BF16)


def exit_kernel(analysed, out, buffer, sent):
    swap = swap_matrix(GROUP)
    core = core_index()
    copies = []
    for start in range(0, HELD, 2 * EIGHT):
        tiles = [
            analysed[home_of(core, p), start : start + 2 * EIGHT, :].astype(F32)
            for p in range(GROUP)
        ]
        for k in range(2):
            first = start + k * EIGHT
            count = min(EIGHT, HELD - first)
            block = jnp.concatenate([tile[k * EIGHT : (k + 1) * EIGHT, :] for tile in tiles], axis=0)
            moved = mm(swap[: count * GROUP, :], block.astype(BF16)).astype(BF16)
            buffer[first : first + count] = moved.reshape(count, GROUP, CORE)
        rows = slice(start, min(start + 2 * EIGHT, HELD))
        copies.append(
            pltpu.make_async_copy(buffer.at[rows], out.at[rows], sent.at[start // (2 * EIGHT)])
        )
        copies[-1].start()
    for copy in copies:
        copy.wait()


def prepare_kernel(
    hosted, tally, taper, location, datum, error_spread, band,
    root_column, ratio_column, root_row, pick,
):
    me = hosted[core_index() * GROUP + lax.axis_index("member")]
    mine = pl.ds(me, 1)
    flat = location[mine, :]
    level = flat >> 5
    column = flat & 31
    spot = level * PIECE_WIDTH + column - FRINGE_REACH
    rim = level * FRINGE_REACH + (column & (FRINGE_REACH - 1))
    spot = jnp.where(column < FRINGE_REACH, CORE + rim, spot)
    spot = jnp.where(column >= FRINGE_REACH + PIECE_WIDTH, CORE + RIM + rim, spot)

    classes = band[mine, :]
    weight = jnp.zeros(classes.shape, I32)
    for k in range(NCLASS):
        weight = jnp.where(classes == k, taper[k], weight)
    slot = lax.broadcasted_iota(I32, classes.shape, 1)
    live = jnp.where(slot < tally[me], 1.0, 0.0)
    precision = live * (weight.astype(F32) / 64.0) / error_spread[mine, :]
    pulled = precision * datum[mine, :]
    for t in range(0, SPAN, 128):
        hit = lax.broadcasted_iota(I32, (128, OBS), 0) + t == spot
        total = jnp.sum(jnp.where(hit, precision, 0.0), axis=1, keepdims=True)
        pull = jnp.sum(jnp.where(hit, pulled, 0.0), axis=1, keepdims=True)
        total = jnp.broadcast_to(total, (128, 128))
        pull = jnp.broadcast_to(pull, (128, 128))
        root = jnp.sqrt(total)
        root_column[t : t + 128, :] = root
        ratio_column[t : t + 128, :] = jnp.where(
            total > 0.0, pull / jnp.where(total > 0.0, root, 1.0), 0.0
        )
        root_row[:, t : t + 128] = root.T[0:8, :]

    row = lax.broadcasted_iota(I32, (2 * RIM, CORE), 0)
    lane = lax.broadcasted_iota(I32, (2 * RIM, CORE), 1)
    rim = jnp.where(row < RIM, row, row - RIM)
    source = (rim >> 3) * PIECE_WIDTH + (rim & (FRINGE_REACH - 1))
    source = jnp.where(row < RIM, source + PIECE_WIDTH - FRINGE_REACH, source)
    pick[...] = jnp.where(lane == source, 1.0, 0.0).astype(BF16)


def extract_kernel(states, pick, rightward, leftward):
    for t in range(0, ROWS, TILE):
        rims = mm_nt(pick[...], states[t : t + TILE, :]).astype(BF16)
        rightward[:, t : t + TILE] = rims[:RIM, :]
        leftward[:, t : t + TILE] = rims[RIM:, :]


def own_kernel(
    states, root_column, ratio_column, root_row,
    spread, state_mean, gram, basis, pulls, sums,
):
    total = jnp.zeros((1, CORE), F32)
    for t in range(0, ROWS, TILE):
        total += jnp.sum(states[t : t + TILE, :].astype(F32), axis=0, keepdims=True)
    mean = total / MEMBERS
    state_mean[...] = jnp.broadcast_to(mean, (8, CORE))
    live = (lax.broadcasted_iota(I32, (TILE, CORE), 0) & (PADDED - 1)) < HELD
    covariance = jnp.zeros((CORE, CORE), F32)
    for t in range(0, ROWS, TILE):
        tile = jnp.where(live, states[t : t + TILE, :].astype(F32) - mean, 0.0)
        spread[t : t + TILE, :] = tile.astype(BF16)
        covariance += mm(tile.T.astype(BF16), tile.astype(BF16))
    squares = jnp.zeros((1, 1), F32)
    trace = jnp.zeros((1, 1), F32)
    corner = lax.broadcasted_iota(I32, (128, 128), 0) == lax.broadcasted_iota(I32, (128, 128), 1)
    column_mean = jnp.broadcast_to(mean, (128, CORE)).T
    for t in range(0, CORE, 128):
        root = root_column[t : t + 128, :]
        lifted = jnp.tile(root, (1, CORE // 128)) * covariance[t : t + 128, :]
        basis[t : t + 128, :] = lifted
        block = lifted * root_row[0:1, :CORE]
        gram[t : t + 128, :] = block.astype(BF16)
        squares += jnp.sum(block * block, keepdims=True)
        trace += jnp.sum(jnp.where(corner, block[:, t : t + 128], 0.0), keepdims=True)
        pulls[t : t + 128, :] = ratio_column[t : t + 128, :] - root * column_mean[t : t + 128, :]
    sums[0:8, :] = jnp.broadcast_to(squares, (8, 128))
    sums[8:16, :] = jnp.broadcast_to(trace, (8, 128))


def analyse_kernel(
    before, after, spread, state_mean, own_gram, own_basis, own_pulls, sums,
    root_column, ratio_column, root_row,
    out, fringe_t, fringe, gram, basis, pulls, first, second, third, fourth,
):
    live = (lax.broadcasted_iota(I32, (RIM, ROWS), 1) & (PADDED - 1)) < HELD
    for rims, top in ((before, 0), (after, RIM)):
        rows = slice(top, top + RIM)
        tile = rims[...].astype(F32)
        mean = jnp.sum(tile, axis=1, keepdims=True) / MEMBERS
        fringe_t[rows, :] = jnp.where(live, tile - mean, 0.0).astype(BF16)
        span = slice(CORE + top, CORE + top + RIM)
        pulls[span, :] = ratio_column[span, :] - root_column[span, :] * mean
    pulls[:CORE, :] = own_pulls[...]
    gram[:CORE, :CORE] = own_gram[...]
    basis[:CORE, :] = own_basis[...]
    first[:CORE, :CORE] = own_basis[...].astype(BF16)
    first[:, CORE:] = pulls[...].astype(BF16)

    corner = lax.broadcasted_iota(I32, (128, 128), 0) == lax.broadcasted_iota(I32, (128, 128), 1)
    squares = sums[0:1, 0:1]
    trace = sums[8:9, 0:1]
    for t in range(0, CORE, 128):
        rows = slice(CORE + t, CORE + t + 128)
        root = jnp.tile(root_column[rows, :], (1, CORE // 128))
        strip = fringe_t[t : t + 128, :]
        lifted = root * mm(strip, spread[...])
        basis[rows, :] = lifted
        first[rows, :CORE] = lifted.astype(BF16)
        block = lifted * root_row[0:1, :CORE]
        gram[rows, :CORE] = block.astype(BF16)
        gram[:CORE, rows] = block.astype(BF16).T
        squares += 2.0 * jnp.sum(block * block, keepdims=True)
        block = root * mm_nt(strip, fringe_t[...]) * root_row[0:1, CORE:]
        gram[rows, CORE:] = block.astype(BF16)
        squares += jnp.sum(block * block, keepdims=True)
        trace += jnp.sum(jnp.where(corner, block[:, t : t + 128], 0.0), keepdims=True)
    draw = F32(MEMBERS - 1)
    inverse = 1.0 / (draw + 2.0 * squares / (draw + trace))

    a = draw * inverse
    r = 1.5 - 0.5 * a
    s = 1.5 - 0.5 * a * r * r

    def step(source):
        product = mm(gram[...], source[...])
        return product[:, :CORE], product[:, CORE:]

    def turn(t):
        fringe[:, t : t + 128] = fringe_t[t : t + 128, :].T

    turn(0)
    pv, px = step(first)
    v = (0.25 * inverse * inverse) * pv - (r * inverse) * basis[...]
    second[:, :CORE] = v.astype(BF16)
    second[:, CORE:] = (r * pulls[...] - (0.5 * inverse) * px).astype(BF16)

    turn(128)
    pv, px = step(second)
    v = (0.5 * a) * second[:, :CORE].astype(F32) + (0.5 * inverse) * pv
    v += (0.5 * r * r * inverse) * basis[...]
    third[:, :CORE] = (-v).astype(BF16)
    x = r * second[:, CORE:].astype(F32) - (0.5 * inverse) * px
    third[:, CORE:] = x.astype(BF16)

    turn(256)
    pv, px = step(third)
    v = r * third[:, :CORE].astype(F32) - (0.5 * inverse) * pv
    v -= (0.5 * s * inverse) * basis[...]
    fourth[:, :CORE] = v.astype(BF16)
    x = (0.5 * a) * third[:, CORE:].astype(F32) + (0.5 * inverse) * px
    fourth[:, CORE:] = (1.5 * pulls[...] - x).astype(BF16)
    first[:, :CORE] = (jnp.tile(root_column[...], (1, CORE // 128)) * v).astype(BF16)

    pv, px = step(fourth)
    x = inverse * (r * fourth[:, CORE:].astype(F32) - (0.5 * inverse) * px)
    shift = []
    for t in range(0, CORE, 128):
        both = (r * s) * basis[:, t : t + 128] + pv[:, t : t + 128]
        shift.append(jnp.sum(x * both, axis=0, keepdims=True))
    base = state_mean[0:1, :] + jnp.concatenate(shift, axis=1)
    gain = jnp.sqrt(a)
    for t in range(0, ROWS, TILE):
        own = spread[t : t + TILE, :]
        moved = mm(own, first[:CORE, :CORE]) + mm(fringe[t : t + TILE, :], first[CORE:, :CORE])
        moved += r * s * own.astype(F32)
        out[t : t + TILE, :] = (base + gain * moved).astype(BF16)


def call(kernel, name, in_specs, out_shape, out_specs=None, scratch_shapes=(), flops=0):
    return pl.pallas_call(
        kernel,
        in_specs=in_specs,
        out_specs=out_specs or jax.tree.map(lambda _: vmem(), out_shape),
        out_shape=out_shape,
        scratch_shapes=list(scratch_shapes),
        compiler_params=params(),
        cost_estimate=pl.CostEstimate(flops=flops, bytes_accessed=1 << 20, transcendentals=0),
        name=name,
    )


def enter(states):
    return call(
        entry_kernel, "entry", [vmem()], shape(GROUP, PADDED, CORE), flops=8 * 256 * 256 * CORE
    )(states)


def leave(analysed):
    return call(
        exit_kernel, "exit", [vmem()], shape(HELD, GROUP, CORE), hbm(),
        [pltpu.VMEM((HELD, GROUP, CORE), BF16), pltpu.SemaphoreType.DMA((2,))],
        8 * 256 * 256 * CORE,
    )(analysed)


def prepare(hosted, tally, taper, location, datum, error_spread, band):
    return call(
        prepare_kernel, "prepare", [smem()] * 3 + [vmem()] * 4,
        [shape(SPAN, 128, dtype=F32), shape(SPAN, 128, dtype=F32), shape(8, SPAN, dtype=F32),
         shape(2 * RIM, CORE)],
        flops=4 * SPAN * OBS,
    )(hosted, tally, taper, location, datum, error_spread, band)


def extract(states, pick):
    return call(
        extract_kernel, "extract", [vmem()] * 2, [shape(RIM, ROWS), shape(RIM, ROWS)],
        flops=4 * RIM * CORE * ROWS,
    )(states, pick)


def own_part(states, root_column, ratio_column, root_row):
    return call(
        own_kernel, "own_part", [vmem()] * 4,
        [shape(ROWS, CORE), shape(8, CORE, dtype=F32), shape(CORE, CORE),
         shape(CORE, CORE, dtype=F32), shape(CORE, 128, dtype=F32), shape(16, 128, dtype=F32)],
        flops=2 * ROWS * CORE * CORE,
    )(states, root_column, ratio_column, root_row)


def analyse(before, after, own, prepared):
    chain = pltpu.VMEM((SPAN, CORE + 128), BF16)
    return call(
        analyse_kernel, "analyse", [vmem()] * 11, shape(ROWS, CORE),
        scratch_shapes=[
            pltpu.VMEM((CORE, ROWS), BF16),
            pltpu.VMEM((ROWS, CORE), BF16),
            pltpu.VMEM((SPAN, SPAN), BF16),
            pltpu.VMEM((SPAN, CORE), F32),
            pltpu.VMEM((SPAN, 128), F32),
            chain, chain, chain, chain,
        ],
        flops=8 * SPAN * SPAN * CORE,
    )(before, after, *own, *prepared)


def local(
    background_fields,
    measured_location,
    measured_datum,
    measured_error_spread,
    measured_distance_band,
    measured_tally,
    taper_weights,
):
    axes = ("member", "patch")
    groups = lax.axis_size("patch")
    sent = enter(jnp.transpose(background_fields, (1, 0, 2)))
    received = lax.all_to_all(sent, "member", split_axis=0, concat_axis=0, tiled=True)
    *prepared, pick = prepare(
        jnp.asarray(HOSTED), measured_tally, taper_weights, measured_location, measured_datum,
        measured_error_spread, measured_distance_band,
    )
    states = received.reshape(ROWS, CORE)
    rightward, leftward = extract(states, pick)
    owners = [CYCLES[g % 2][p] * groups + g for g in range(groups) for p in range(GROUP)]
    up = list(zip(owners, owners[1:] + owners[:1]))
    down = [(j, i) for i, j in up]
    before = lax.ppermute(rightward, axes, up)
    after = lax.ppermute(leftward, axes, down)
    own = own_part(states, *prepared)
    analysed = analyse(before, after, own, prepared).reshape(GROUP, PADDED, CORE)
    returned = lax.all_to_all(analysed, "member", split_axis=0, concat_axis=0, tiled=True)
    return jnp.transpose(leave(returned), (1, 0, 2))


def solution(mesh):
    placed = (
        P("patch", "member", None),
        P("patch", None),
        P("patch", None),
        P("patch", None),
        P("patch", None),
        P("patch"),
        P(),
    )
    return jax.shard_map(
        local, mesh=mesh, in_specs=placed, out_specs=P("patch", "member", None), check_vma=False
    )
```

```python
import jax
import jax.numpy as jnp
import numpy as np
from jax import lax
from jax.experimental import pallas as pl
from jax.experimental.pallas import tpu as pltpu
from jax.sharding import PartitionSpec as P

STRATUM_PAIRS = 24
PIECE_WIDTH = 16
FRINGE_REACH = 8
NCLASS = 16
CORE = STRATUM_PAIRS * PIECE_WIDTH
RIM = STRATUM_PAIRS * FRINGE_REACH
SPAN = CORE + 2 * RIM
OBS = 640
GROUP = 32
HELD = 30
PADDED = 32
ROWS = GROUP * PADDED
MEMBERS = GROUP * HELD
EIGHT = 8
TILE = 256

F32 = jnp.float32
BF16 = jnp.bfloat16
I32 = jnp.int32

CYCLES = (
    (0, 8, 9, 17, 16, 23, 22, 14, 15, 7, 6, 5, 13, 21, 20, 12,
     4, 3, 2, 1, 25, 26, 18, 10, 11, 19, 27, 28, 29, 30, 31, 24),
    (0, 1, 9, 10, 2, 26, 27, 3, 11, 12, 13, 14, 6, 30, 22, 21,
     29, 5, 4, 28, 20, 19, 18, 17, 25, 24, 16, 8, 15, 23, 31, 7),
)
HOSTED = np.argsort(np.array(CYCLES, np.int32), axis=1).astype(np.int32).reshape(-1)


def vmem():
    return pl.BlockSpec(memory_space=pltpu.VMEM)


def smem():
    return pl.BlockSpec(memory_space=pltpu.SMEM)


def hbm():
    return pl.BlockSpec(memory_space=pltpu.HBM)


def params():
    return pltpu.CompilerParams(vmem_limit_bytes=40 * 1024 * 1024)


def shape(*dims, dtype=BF16):
    return jax.ShapeDtypeStruct(dims, dtype)


def mm(a, b):
    return jnp.dot(a, b, preferred_element_type=F32)


def mm_nt(a, b):
    return lax.dot_general(a, b, (((1,), (1,)), ((), ())), preferred_element_type=F32)


def swap_matrix(inner):
    size = GROUP * EIGHT
    row = lax.broadcasted_iota(I32, (size, size), 0)
    column = lax.broadcasted_iota(I32, (size, size), 1)
    wanted = (row & (inner - 1)) * (size // inner) + row // inner
    return jnp.where(column == wanted, 1.0, 0.0).astype(BF16)


def core_index():
    return lax.axis_index("patch") % 2


def home_of(core, patch):
    return jnp.where(core == 0, CYCLES[0][patch], CYCLES[1][patch])


def entry_kernel(states, out):
    swap = swap_matrix(EIGHT)
    core = core_index()
    for start in range(0, HELD, 2 * EIGHT):
        halves = []
        for first in (start, start + EIGHT):
            count = min(EIGHT, HELD - first)
            block = states[first : first + count].reshape(count * GROUP, CORE)
            halves.append(mm(swap[:, : count * GROUP], block))
        for p in range(GROUP):
            rows = slice(p * EIGHT, (p + 1) * EIGHT)
            both = jnp.concatenate([half[rows, :] for half in halves], axis=0)
            out[home_of(core, p), start : start + 2 * EIGHT, :] = both.astype(BF16)


def exit_kernel(analysed, out, buffer, sent):
    swap = swap_matrix(GROUP)
    core = core_index()
    copies = []
    for start in range(0, HELD, 2 * EIGHT):
        tiles = [
            analysed[home_of(core, p), start : start + 2 * EIGHT, :].astype(F32)
            for p in range(GROUP)
        ]
        for k in range(2):
            first = start + k * EIGHT
            count = min(EIGHT, HELD - first)
            block = jnp.concatenate([tile[k * EIGHT : (k + 1) * EIGHT, :] for tile in tiles], axis=0)
            moved = mm(swap[: count * GROUP, :], block.astype(BF16)).astype(BF16)
            buffer[first : first + count] = moved.reshape(count, GROUP, CORE)
        rows = slice(start, min(start + 2 * EIGHT, HELD))
        copies.append(
            pltpu.make_async_copy(buffer.at[rows], out.at[rows], sent.at[start // (2 * EIGHT)])
        )
        copies[-1].start()
    for copy in copies:
        copy.wait()


def prepare_kernel(
    hosted, tally, taper, location, datum, error_spread, band,
    root_column, ratio_column, root_row, pick,
):
    me = hosted[core_index() * GROUP + lax.axis_index("member")]
    mine = pl.ds(me, 1)
    flat = location[mine, :]
    level = flat >> 5
    column = flat & 31
    spot = level * PIECE_WIDTH + column - FRINGE_REACH
    rim = level * FRINGE_REACH + (column & (FRINGE_REACH - 1))
    spot = jnp.where(column < FRINGE_REACH, CORE + rim, spot)
    spot = jnp.where(column >= FRINGE_REACH + PIECE_WIDTH, CORE + RIM + rim, spot)

    classes = band[mine, :]
    weight = jnp.zeros(classes.shape, I32)
    for k in range(NCLASS):
        weight = jnp.where(classes == k, taper[k], weight)
    slot = lax.broadcasted_iota(I32, classes.shape, 1)
    live = jnp.where(slot < tally[me], 1.0, 0.0)
    precision = live * (weight.astype(F32) / 64.0) / error_spread[mine, :]
    pulled = precision * datum[mine, :]
    for t in range(0, SPAN, 128):
        hit = lax.broadcasted_iota(I32, (128, OBS), 0) + t == spot
        total = jnp.sum(jnp.where(hit, precision, 0.0), axis=1, keepdims=True)
        pull = jnp.sum(jnp.where(hit, pulled, 0.0), axis=1, keepdims=True)
        total = jnp.broadcast_to(total, (128, 128))
        pull = jnp.broadcast_to(pull, (128, 128))
        root = jnp.sqrt(total)
        root_column[t : t + 128, :] = root
        ratio_column[t : t + 128, :] = jnp.where(
            total > 0.0, pull / jnp.where(total > 0.0, root, 1.0), 0.0
        )
        root_row[:, t : t + 128] = root.T[0:8, :]

    row = lax.broadcasted_iota(I32, (2 * RIM, CORE), 0)
    lane = lax.broadcasted_iota(I32, (2 * RIM, CORE), 1)
    rim = jnp.where(row < RIM, row, row - RIM)
    source = (rim >> 3) * PIECE_WIDTH + (rim & (FRINGE_REACH - 1))
    source = jnp.where(row < RIM, source + PIECE_WIDTH - FRINGE_REACH, source)
    pick[...] = jnp.where(lane == source, 1.0, 0.0).astype(BF16)


def extract_kernel(states, pick, rightward, leftward):
    for t in range(0, ROWS, TILE):
        rims = mm_nt(pick[...], states[t : t + TILE, :]).astype(BF16)
        rightward[:, t : t + TILE] = rims[:RIM, :]
        leftward[:, t : t + TILE] = rims[RIM:, :]


def corners(block):
    same = lax.broadcasted_iota(I32, block.shape, 0) == lax.broadcasted_iota(I32, block.shape, 1)
    return jnp.sum(jnp.where(same, block, 0.0), keepdims=True)


def squared(block):
    return jnp.sum(block * block, keepdims=True)


def own_kernel(
    states, root_column, ratio_column, root_row,
    window, gram, basis, first, pulls, state_mean, sums,
):
    total = jnp.zeros((1, CORE), F32)
    for t in range(0, ROWS, TILE):
        total += jnp.sum(states[t : t + TILE, :].astype(F32), axis=0, keepdims=True)
    mean = total / MEMBERS
    state_mean[...] = jnp.broadcast_to(mean, (8, CORE))
    live = (lax.broadcasted_iota(I32, (TILE, CORE), 0) & (PADDED - 1)) < HELD
    covariance = jnp.zeros((CORE, CORE), F32)
    for t in range(0, ROWS, TILE):
        tile = jnp.where(live, states[t : t + TILE, :].astype(F32) - mean, 0.0)
        window[t : t + TILE, :CORE] = tile.astype(BF16)
        covariance += mm(tile.T.astype(BF16), tile.astype(BF16))
    root = root_column[:CORE, :]
    lifted = jnp.tile(root, (1, CORE // 128)) * covariance
    basis[:CORE, :] = lifted
    first[:CORE, :CORE] = lifted.astype(BF16)
    block = lifted * root_row[0:1, :CORE]
    gram[:CORE, :CORE] = block.astype(BF16)
    pull = ratio_column[:CORE, :] - root * jnp.broadcast_to(mean, (128, CORE)).T
    pulls[:CORE, :] = pull
    first[:CORE, CORE:] = pull.astype(BF16)
    sums[0:8, :] = jnp.broadcast_to(squared(block), (8, 128))
    sums[8:16, :] = jnp.broadcast_to(corners(block), (8, 128))


def add_rim(rims, top, earlier, root_column, ratio_column, root_row, window, gram, basis, first, pulls):
    span = slice(top, top + RIM)
    live = (lax.broadcasted_iota(I32, (RIM, ROWS), 1) & (PADDED - 1)) < HELD
    tile = rims[...].astype(F32)
    mean = jnp.sum(tile, axis=1, keepdims=True) / MEMBERS
    strip = jnp.where(live, tile - mean, 0.0).astype(BF16)
    narrow = root_column[span, :]
    pull = ratio_column[span, :] - narrow * mean
    pulls[span, :] = pull
    first[span, CORE:] = pull.astype(BF16)
    lifted = jnp.tile(narrow, (1, CORE // 128)) * mm(strip, window[:, :CORE])
    basis[span, :] = lifted
    first[span, :CORE] = lifted.astype(BF16)
    block = lifted * root_row[0:1, :CORE]
    gram[span, :CORE] = block.astype(BF16)
    gram[:CORE, span] = block.astype(BF16).T
    squares = 2.0 * squared(block)
    root = root_column[span, 0:1]
    if earlier is not None:
        block = root * mm_nt(strip, earlier[...]) * root_row[0:1, CORE : CORE + RIM]
        gram[span, CORE : CORE + RIM] = block.astype(BF16)
        gram[CORE : CORE + RIM, span] = block.astype(BF16).T
        squares += 2.0 * squared(block)
    block = root * mm_nt(strip, strip) * root_row[0:1, span]
    gram[span, span] = block.astype(BF16)
    return strip, squares + squared(block), corners(block)


def before_kernel(
    before, own_sums, root_column, ratio_column, root_row, _window, _gram, _basis, _first, _pulls,
    window, gram, basis, first, pulls, strip, sums,
):
    added, squares, trace = add_rim(
        before, CORE, None, root_column, ratio_column, root_row, window, gram, basis, first, pulls
    )
    strip[...] = added
    window[:, CORE : CORE + RIM] = added.T
    sums[0:8, :] = own_sums[0:8, :] + squares
    sums[8:16, :] = own_sums[8:16, :] + trace


def analyse_kernel(
    after, strip, state_mean, sums, root_column, ratio_column, root_row,
    _window, _gram, _basis, _first, _pulls,
    window, gram, basis, first, pulls, out, second, third, fourth,
):
    added, squares, trace = add_rim(
        after, CORE + RIM, strip, root_column, ratio_column, root_row, window, gram, basis, first,
        pulls,
    )
    squares += sums[0:1, 0:1]
    trace += sums[8:9, 0:1]
    draw = F32(MEMBERS - 1)
    inverse = 1.0 / (draw + 2.0 * squares / (draw + trace))

    a = draw * inverse
    r = 1.5 - 0.5 * a
    s = 1.5 - 0.5 * a * r * r
    halves = ((slice(0, 256), slice(0, 256)), (slice(256, CORE), slice(0, 128)))
    last = slice(CORE, CORE + 128)

    def product(source, h):
        return mm(gram[...], source[:, h * 256 : (h + 1) * 256])

    def one(h, p):
        wide, part = halves[h]
        v = (0.25 * inverse * inverse) * p[:, part] - (r * inverse) * basis[:, wide]
        second[:, wide] = v.astype(BF16)
        if h:
            second[:, last] = (r * pulls[...] - (0.5 * inverse) * p[:, 128:]).astype(BF16)

    def two(h, p):
        wide, part = halves[h]
        v = (-0.5 * a) * second[:, wide].astype(F32) - (0.5 * inverse) * p[:, part]
        v -= (0.5 * r * r * inverse) * basis[:, wide]
        third[:, wide] = v.astype(BF16)
        if h:
            x = r * second[:, last].astype(F32) - (0.5 * inverse) * p[:, 128:]
            third[:, last] = x.astype(BF16)

    def three(h, p):
        wide, part = halves[h]
        v = r * third[:, wide].astype(F32) - (0.5 * inverse) * p[:, part]
        v -= (0.5 * s * inverse) * basis[:, wide]
        fourth[:, wide] = v.astype(BF16)
        first[:, wide] = (jnp.tile(root_column[...], (1, v.shape[1] // 128)) * v).astype(BF16)
        if h:
            x = (-0.5 * a) * third[:, last].astype(F32) - (0.5 * inverse) * p[:, 128:]
            fourth[:, last] = (1.5 * pulls[...] + x).astype(BF16)

    chain = (first, second, third, fourth)
    waiting = [product(first, 0), product(first, 1)]
    window[:, CORE + RIM :] = added.T
    for k, finish in enumerate((one, two, three)):
        for h in range(2):
            finish(h, waiting[h])
            waiting[h] = product(chain[k + 1], h)
    x = r * fourth[:, last].astype(F32) - (0.5 * inverse) * waiting[1][:, 128:]
    x *= inverse
    shift = []
    for h, (wide, part) in enumerate(halves):
        for t in range(part.start, part.stop, 128):
            both = (r * s) * basis[:, h * 256 + t : h * 256 + t + 128] + waiting[h][:, t : t + 128]
            shift.append(jnp.sum(x * both, axis=0, keepdims=True))
    base = state_mean[0:1, :] + jnp.concatenate(shift, axis=1)
    gain = jnp.sqrt(a)
    for t in range(0, ROWS, TILE):
        rows = slice(t, t + TILE)
        moved = mm(window[rows, :], first[:, :CORE])
        moved += r * s * window[rows, :CORE].astype(F32)
        out[rows, :] = (base + gain * moved).astype(BF16)


def call(
    kernel, name, in_specs, out_shape, out_specs=None, scratch_shapes=(), flops=0, aliases=None
):
    return pl.pallas_call(
        kernel,
        in_specs=in_specs,
        out_specs=out_specs or jax.tree.map(lambda _: vmem(), out_shape),
        out_shape=out_shape,
        scratch_shapes=list(scratch_shapes),
        input_output_aliases=aliases or {},
        compiler_params=params(),
        cost_estimate=pl.CostEstimate(flops=flops, bytes_accessed=1 << 20, transcendentals=0),
        name=name,
    )


def enter(states):
    return call(
        entry_kernel, "entry", [vmem()], shape(GROUP, PADDED, CORE), flops=8 * 256 * 256 * CORE
    )(states)


def leave(analysed):
    return call(
        exit_kernel, "exit", [vmem()], shape(HELD, GROUP, CORE), hbm(),
        [pltpu.VMEM((HELD, GROUP, CORE), BF16), pltpu.SemaphoreType.DMA((2,))],
        8 * 256 * 256 * CORE,
    )(analysed)


def prepare(hosted, tally, taper, location, datum, error_spread, band):
    return call(
        prepare_kernel, "prepare", [smem()] * 3 + [vmem()] * 4,
        [shape(SPAN, 128, dtype=F32), shape(SPAN, 128, dtype=F32), shape(8, SPAN, dtype=F32),
         shape(2 * RIM, CORE)],
        flops=4 * SPAN * OBS,
    )(hosted, tally, taper, location, datum, error_spread, band)


def extract(states, pick):
    return call(
        extract_kernel, "extract", [vmem()] * 2, [shape(RIM, ROWS), shape(RIM, ROWS)],
        flops=4 * RIM * CORE * ROWS,
    )(states, pick)


def growing():
    return [
        shape(ROWS, SPAN), shape(SPAN, SPAN), shape(SPAN, CORE, dtype=F32),
        shape(SPAN, CORE + 128), shape(SPAN, 128, dtype=F32),
    ]


def own_part(states, prepared):
    *grown, state_mean, sums = call(
        own_kernel, "own_part", [vmem()] * 4,
        growing() + [shape(8, CORE, dtype=F32), shape(16, 128, dtype=F32)],
        flops=2 * ROWS * CORE * CORE,
    )(states, *prepared)
    return grown, state_mean, sums


def before_part(before, grown, sums, prepared):
    *grown, strip, sums = call(
        before_kernel, "before_part", [vmem()] * 10,
        growing() + [shape(RIM, ROWS), shape(16, 128, dtype=F32)],
        flops=2 * ROWS * RIM * (CORE + RIM), aliases={5 + k: k for k in range(5)},
    )(before, sums, *prepared, *grown)
    return grown, strip, sums


def analyse(after, grown, strip, state_mean, sums, prepared):
    chain = pltpu.VMEM((SPAN, CORE + 128), BF16)
    return call(
        analyse_kernel, "analyse", [vmem()] * 12, growing() + [shape(ROWS, CORE)],
        scratch_shapes=[chain, chain, chain],
        flops=8 * SPAN * SPAN * CORE, aliases={7 + k: k for k in range(5)},
    )(after, strip, state_mean, sums, *prepared, *grown)[-1]


def local(
    background_fields,
    measured_location,
    measured_datum,
    measured_error_spread,
    measured_distance_band,
    measured_tally,
    taper_weights,
):
    axes = ("member", "patch")
    groups = lax.axis_size("patch")
    sent = enter(jnp.transpose(background_fields, (1, 0, 2)))
    received = lax.all_to_all(sent, "member", split_axis=0, concat_axis=0, tiled=True)
    *prepared, pick = prepare(
        jnp.asarray(HOSTED), measured_tally, taper_weights, measured_location, measured_datum,
        measured_error_spread, measured_distance_band,
    )
    states = received.reshape(ROWS, CORE)
    rightward, leftward = extract(states, pick)
    owners = [CYCLES[g % 2][p] * groups + g for g in range(groups) for p in range(GROUP)]
    up = list(zip(owners, owners[1:] + owners[:1]))
    down = [(j, i) for i, j in up]
    before = lax.ppermute(rightward, axes, up)
    after = lax.ppermute(leftward, axes, down)
    grown, state_mean, sums = own_part(states, prepared)
    grown, strip, sums = before_part(before, grown, sums, prepared)
    analysed = analyse(after, grown, strip, state_mean, sums, prepared)
    analysed = analysed.reshape(GROUP, PADDED, CORE)
    returned = lax.all_to_all(analysed, "member", split_axis=0, concat_axis=0, tiled=True)
    return jnp.transpose(leave(returned), (1, 0, 2))


def solution(mesh):
    placed = (
        P("patch", "member", None),
        P("patch", None),
        P("patch", None),
        P("patch", None),
        P("patch", None),
        P("patch"),
        P(),
    )
    return jax.shard_map(
        local, mesh=mesh, in_specs=placed, out_specs=P("patch", "member", None), check_vma=False
    )
```

```python
import jax
import jax.numpy as jnp
import numpy as np
from jax import lax
from jax.experimental import pallas as pl
from jax.experimental.pallas import tpu as pltpu
from jax.sharding import PartitionSpec as P

STRATUM_PAIRS = 24
PIECE_WIDTH = 16
FRINGE_REACH = 8
NCLASS = 16
CORE = STRATUM_PAIRS * PIECE_WIDTH
RIM = STRATUM_PAIRS * FRINGE_REACH
SPAN = CORE + 2 * RIM
OBS = 640
GROUP = 32
HELD = 30
PADDED = 32
ROWS = GROUP * PADDED
MEMBERS = GROUP * HELD
EIGHT = 8
TILE = 256

F32 = jnp.float32
BF16 = jnp.bfloat16
I32 = jnp.int32

CYCLES = (
    (0, 8, 9, 17, 16, 23, 22, 14, 15, 7, 6, 5, 13, 21, 20, 12,
     4, 3, 2, 1, 25, 26, 18, 10, 11, 19, 27, 28, 29, 30, 31, 24),
    (0, 1, 9, 10, 2, 26, 27, 3, 11, 12, 13, 14, 6, 30, 22, 21,
     29, 5, 4, 28, 20, 19, 18, 17, 25, 24, 16, 8, 15, 23, 31, 7),
)
HOSTED = np.argsort(np.array(CYCLES, np.int32), axis=1).astype(np.int32).reshape(-1)


def vmem():
    return pl.BlockSpec(memory_space=pltpu.VMEM)


def smem():
    return pl.BlockSpec(memory_space=pltpu.SMEM)


def hbm():
    return pl.BlockSpec(memory_space=pltpu.HBM)


def params():
    return pltpu.CompilerParams(vmem_limit_bytes=40 * 1024 * 1024)


def shape(*dims, dtype=BF16):
    return jax.ShapeDtypeStruct(dims, dtype)


def mm(a, b):
    return jnp.dot(a, b, preferred_element_type=F32)


def mm_nt(a, b):
    return lax.dot_general(a, b, (((1,), (1,)), ((), ())), preferred_element_type=F32)


def swap_matrix(inner):
    size = GROUP * EIGHT
    row = lax.broadcasted_iota(I32, (size, size), 0)
    column = lax.broadcasted_iota(I32, (size, size), 1)
    wanted = (row & (inner - 1)) * (size // inner) + row // inner
    return jnp.where(column == wanted, 1.0, 0.0).astype(BF16)


def core_index():
    return lax.axis_index("patch") % 2


def home_of(core, patch):
    return jnp.where(core == 0, CYCLES[0][patch], CYCLES[1][patch])


def entry_kernel(states, out):
    swap = swap_matrix(EIGHT)
    core = core_index()
    for start in range(0, HELD, 2 * EIGHT):
        halves = []
        for first in (start, start + EIGHT):
            count = min(EIGHT, HELD - first)
            block = states[first : first + count].reshape(count * GROUP, CORE)
            halves.append(mm(swap[:, : count * GROUP], block))
        for p in range(GROUP):
            rows = slice(p * EIGHT, (p + 1) * EIGHT)
            both = jnp.concatenate([half[rows, :] for half in halves], axis=0)
            out[home_of(core, p), start : start + 2 * EIGHT, :] = both.astype(BF16)


def exit_kernel(analysed, out, buffer, sent):
    swap = swap_matrix(GROUP)
    core = core_index()
    copies = []
    for start in range(0, HELD, 2 * EIGHT):
        tiles = [
            analysed[home_of(core, p), start : start + 2 * EIGHT, :].astype(F32)
            for p in range(GROUP)
        ]
        for k in range(2):
            first = start + k * EIGHT
            count = min(EIGHT, HELD - first)
            block = jnp.concatenate([tile[k * EIGHT : (k + 1) * EIGHT, :] for tile in tiles], axis=0)
            moved = mm(swap[: count * GROUP, :], block.astype(BF16)).astype(BF16)
            buffer[first : first + count] = moved.reshape(count, GROUP, CORE)
        rows = slice(start, min(start + 2 * EIGHT, HELD))
        copies.append(
            pltpu.make_async_copy(buffer.at[rows], out.at[rows], sent.at[start // (2 * EIGHT)])
        )
        copies[-1].start()
    for copy in copies:
        copy.wait()


def prepare_kernel(
    hosted, tally, taper, location, datum, error_spread, band,
    root_column, ratio_column, root_row, pick,
):
    me = hosted[core_index() * GROUP + lax.axis_index("member")]
    mine = pl.ds(me, 1)
    flat = location[mine, :]
    level = flat >> 5
    column = flat & 31
    spot = level * PIECE_WIDTH + column - FRINGE_REACH
    rim = level * FRINGE_REACH + (column & (FRINGE_REACH - 1))
    spot = jnp.where(column < FRINGE_REACH, CORE + rim, spot)
    spot = jnp.where(column >= FRINGE_REACH + PIECE_WIDTH, CORE + RIM + rim, spot)

    classes = band[mine, :]
    weight = jnp.zeros(classes.shape, I32)
    for k in range(NCLASS):
        weight = jnp.where(classes == k, taper[k], weight)
    slot = lax.broadcasted_iota(I32, classes.shape, 1)
    live = jnp.where(slot < tally[me], 1.0, 0.0)
    precision = live * (weight.astype(F32) / 64.0) / error_spread[mine, :]
    pulled = precision * datum[mine, :]
    for t in range(0, SPAN, 128):
        hit = lax.broadcasted_iota(I32, (128, OBS), 0) + t == spot
        total = jnp.sum(jnp.where(hit, precision, 0.0), axis=1, keepdims=True)
        pull = jnp.sum(jnp.where(hit, pulled, 0.0), axis=1, keepdims=True)
        total = jnp.broadcast_to(total, (128, 128))
        pull = jnp.broadcast_to(pull, (128, 128))
        root = jnp.sqrt(total)
        root_column[t : t + 128, :] = root
        ratio_column[t : t + 128, :] = jnp.where(
            total > 0.0, pull / jnp.where(total > 0.0, root, 1.0), 0.0
        )
        root_row[:, t : t + 128] = root.T[0:8, :]

    row = lax.broadcasted_iota(I32, (2 * RIM, CORE), 0)
    lane = lax.broadcasted_iota(I32, (2 * RIM, CORE), 1)
    rim = jnp.where(row < RIM, row, row - RIM)
    source = (rim >> 3) * PIECE_WIDTH + (rim & (FRINGE_REACH - 1))
    source = jnp.where(row < RIM, source + PIECE_WIDTH - FRINGE_REACH, source)
    pick[...] = jnp.where(lane == source, 1.0, 0.0).astype(BF16)


def extract_kernel(states, pick, rightward, leftward):
    for t in range(0, ROWS, TILE):
        rims = mm_nt(pick[...], states[t : t + TILE, :]).astype(BF16)
        rightward[:, t : t + TILE] = rims[:RIM, :]
        leftward[:, t : t + TILE] = rims[RIM:, :]


def corners(block):
    same = lax.broadcasted_iota(I32, block.shape, 0) == lax.broadcasted_iota(I32, block.shape, 1)
    return jnp.sum(jnp.where(same, block, 0.0), keepdims=True)


def squared(block):
    return jnp.sum(block * block, keepdims=True)


def scales(peak):
    exponent = jnp.floor(jnp.log2(jnp.where(peak > 0.0, peak, 1.0)))
    exponent = jnp.minimum(jnp.maximum(exponent, -100.0), 120.0)
    return jnp.exp2(exponent), jnp.exp2(-exponent)


def own_kernel(
    states, root_column, ratio_column, root_row,
    window, gram, basis, first, pulls, weight_column, weight_row, state_mean, sums,
):
    total = jnp.zeros((1, CORE), F32)
    for t in range(0, ROWS, TILE):
        total += jnp.sum(states[t : t + TILE, :].astype(F32), axis=0, keepdims=True)
    mean = total / MEMBERS
    live = (lax.broadcasted_iota(I32, (TILE, CORE), 0) & (PADDED - 1)) < HELD
    peak = jnp.zeros((1, CORE), F32)
    for t in range(0, ROWS, TILE):
        tile = jnp.where(live, states[t : t + TILE, :].astype(F32) - mean, 0.0)
        peak = jnp.maximum(peak, jnp.max(jnp.abs(tile), axis=0, keepdims=True))
    scale, inverse = scales(peak)
    state_mean[0:1, :] = mean
    state_mean[1:2, :] = scale
    covariance = jnp.zeros((CORE, CORE), F32)
    for t in range(0, ROWS, TILE):
        tile = jnp.where(live, (states[t : t + TILE, :].astype(F32) - mean) * inverse, 0.0)
        window[t : t + TILE, :CORE] = tile.astype(BF16)
        covariance += mm(tile.T.astype(BF16), tile.astype(BF16))
    root = root_column[:CORE, :]
    weight = root * jnp.broadcast_to(scale, (128, CORE)).T
    weight_column[:CORE, :] = weight
    across = root_row[0:1, :CORE] * scale
    weight_row[0:1, :CORE] = across
    lifted = jnp.tile(weight, (1, CORE // 128)) * covariance
    basis[:CORE, :] = lifted
    first[:CORE, :CORE] = lifted.astype(BF16)
    block = lifted * across
    gram[:CORE, :CORE] = block.astype(BF16)
    pull = ratio_column[:CORE, :] - root * jnp.broadcast_to(mean, (128, CORE)).T
    pulls[:CORE, :] = pull
    first[:CORE, CORE:] = pull.astype(BF16)
    sums[0:8, :] = jnp.broadcast_to(squared(block), (8, 128))
    sums[8:16, :] = jnp.broadcast_to(corners(block), (8, 128))


def add_rim(
    rims, top, earlier, root_column, ratio_column,
    window, gram, basis, first, pulls, weight_column, weight_row,
):
    span = slice(top, top + RIM)
    live = (lax.broadcasted_iota(I32, (RIM, ROWS), 1) & (PADDED - 1)) < HELD
    tile = rims[...].astype(F32)
    mean = jnp.sum(tile, axis=1, keepdims=True) / MEMBERS
    tile = jnp.where(live, tile - mean, 0.0)
    scale, inverse = scales(jnp.max(jnp.abs(tile), axis=1, keepdims=True))
    strip = (tile * inverse).astype(BF16)
    root = root_column[span, :]
    pull = ratio_column[span, :] - root * mean
    pulls[span, :] = pull
    first[span, CORE:] = pull.astype(BF16)
    weight = root * scale
    weight_column[span, :] = weight
    across = weight.T[0:1, :]
    weight_row[0:1, span] = across
    lifted = jnp.tile(weight, (1, CORE // 128)) * mm(strip, window[:, :CORE])
    basis[span, :] = lifted
    first[span, :CORE] = lifted.astype(BF16)
    block = lifted * weight_row[0:1, :CORE]
    gram[span, :CORE] = block.astype(BF16)
    gram[:CORE, span] = block.astype(BF16).T
    squares = 2.0 * squared(block)
    weight = weight[:, 0:1]
    if earlier is not None:
        block = weight * mm_nt(strip, earlier[...]) * weight_row[0:1, CORE : CORE + RIM]
        gram[span, CORE : CORE + RIM] = block.astype(BF16)
        gram[CORE : CORE + RIM, span] = block.astype(BF16).T
        squares += 2.0 * squared(block)
    block = weight * mm_nt(strip, strip) * across
    gram[span, span] = block.astype(BF16)
    return strip, squares + squared(block), corners(block)


def before_kernel(
    before, own_sums, root_column, ratio_column,
    _window, _gram, _basis, _first, _pulls, _weight_column, _weight_row,
    window, gram, basis, first, pulls, weight_column, weight_row, strip, sums,
):
    added, squares, trace = add_rim(
        before, CORE, None, root_column, ratio_column,
        window, gram, basis, first, pulls, weight_column, weight_row,
    )
    strip[...] = added
    window[:, CORE : CORE + RIM] = added.T
    sums[0:8, :] = own_sums[0:8, :] + squares
    sums[8:16, :] = own_sums[8:16, :] + trace


def analyse_kernel(
    after, strip, state_mean, sums, root_column, ratio_column,
    _window, _gram, _basis, _first, _pulls, _weight_column, _weight_row,
    window, gram, basis, first, pulls, weight_column, weight_row, out, second, third, fourth,
):
    added, squares, trace = add_rim(
        after, CORE + RIM, strip, root_column, ratio_column,
        window, gram, basis, first, pulls, weight_column, weight_row,
    )
    squares += sums[0:1, 0:1]
    trace += sums[8:9, 0:1]
    draw = F32(MEMBERS - 1)
    inverse = 1.0 / (draw + 2.0 * squares / (draw + trace))

    a = draw * inverse
    r = 1.5 - 0.5 * a
    s = 1.5 - 0.5 * a * r * r
    halves = ((slice(0, 256), slice(0, 256)), (slice(256, CORE), slice(0, 128)))
    last = slice(CORE, CORE + 128)

    def product(source, h):
        return mm(gram[...], source[:, h * 256 : (h + 1) * 256])

    def one(h, p):
        wide, part = halves[h]
        v = (0.25 * inverse * inverse) * p[:, part] - (r * inverse) * basis[:, wide]
        second[:, wide] = v.astype(BF16)
        if h:
            second[:, last] = (r * pulls[...] - (0.5 * inverse) * p[:, 128:]).astype(BF16)

    def two(h, p):
        wide, part = halves[h]
        v = (-0.5 * a) * second[:, wide].astype(F32) - (0.5 * inverse) * p[:, part]
        v -= (0.5 * r * r * inverse) * basis[:, wide]
        third[:, wide] = v.astype(BF16)
        if h:
            x = r * second[:, last].astype(F32) - (0.5 * inverse) * p[:, 128:]
            third[:, last] = x.astype(BF16)

    def three(h, p):
        wide, part = halves[h]
        v = r * third[:, wide].astype(F32) - (0.5 * inverse) * p[:, part]
        v -= (0.5 * s * inverse) * basis[:, wide]
        fourth[:, wide] = v.astype(BF16)
        first[:, wide] = (jnp.tile(weight_column[...], (1, v.shape[1] // 128)) * v).astype(BF16)
        if h:
            x = (-0.5 * a) * third[:, last].astype(F32) - (0.5 * inverse) * p[:, 128:]
            fourth[:, last] = (1.5 * pulls[...] + x).astype(BF16)

    chain = (first, second, third, fourth)
    waiting = [product(first, 0), product(first, 1)]
    window[:, CORE + RIM :] = added.T
    for k, finish in enumerate((one, two, three)):
        for h in range(2):
            finish(h, waiting[h])
            waiting[h] = product(chain[k + 1], h)
    x = r * fourth[:, last].astype(F32) - (0.5 * inverse) * waiting[1][:, 128:]
    x *= inverse
    shift = []
    for h, (wide, part) in enumerate(halves):
        for t in range(part.start, part.stop, 128):
            both = (r * s) * basis[:, h * 256 + t : h * 256 + t + 128] + waiting[h][:, t : t + 128]
            shift.append(jnp.sum(x * both, axis=0, keepdims=True))
    scale = state_mean[1:2, :]
    base = state_mean[0:1, :] + scale * jnp.concatenate(shift, axis=1)
    gain = jnp.sqrt(a) * scale
    for t in range(0, ROWS, TILE):
        rows = slice(t, t + TILE)
        moved = mm(window[rows, :], first[:, :CORE])
        moved += r * s * window[rows, :CORE].astype(F32)
        out[rows, :] = (base + gain * moved).astype(BF16)


def call(
    kernel, name, in_specs, out_shape, out_specs=None, scratch_shapes=(), flops=0, aliases=None
):
    return pl.pallas_call(
        kernel,
        in_specs=in_specs,
        out_specs=out_specs or jax.tree.map(lambda _: vmem(), out_shape),
        out_shape=out_shape,
        scratch_shapes=list(scratch_shapes),
        input_output_aliases=aliases or {},
        compiler_params=params(),
        cost_estimate=pl.CostEstimate(flops=flops, bytes_accessed=1 << 20, transcendentals=0),
        name=name,
    )


def enter(states):
    return call(
        entry_kernel, "entry", [vmem()], shape(GROUP, PADDED, CORE), flops=8 * 256 * 256 * CORE
    )(states)


def leave(analysed):
    return call(
        exit_kernel, "exit", [vmem()], shape(HELD, GROUP, CORE), hbm(),
        [pltpu.VMEM((HELD, GROUP, CORE), BF16), pltpu.SemaphoreType.DMA((2,))],
        8 * 256 * 256 * CORE,
    )(analysed)


def prepare(hosted, tally, taper, location, datum, error_spread, band):
    return call(
        prepare_kernel, "prepare", [smem()] * 3 + [vmem()] * 4,
        [shape(SPAN, 128, dtype=F32), shape(SPAN, 128, dtype=F32), shape(8, SPAN, dtype=F32),
         shape(2 * RIM, CORE)],
        flops=4 * SPAN * OBS,
    )(hosted, tally, taper, location, datum, error_spread, band)


def extract(states, pick):
    return call(
        extract_kernel, "extract", [vmem()] * 2, [shape(RIM, ROWS), shape(RIM, ROWS)],
        flops=4 * RIM * CORE * ROWS,
    )(states, pick)


def growing():
    return [
        shape(ROWS, SPAN), shape(SPAN, SPAN), shape(SPAN, CORE, dtype=F32),
        shape(SPAN, CORE + 128), shape(SPAN, 128, dtype=F32),
        shape(SPAN, 128, dtype=F32), shape(8, SPAN, dtype=F32),
    ]


def own_part(states, prepared):
    *grown, state_mean, sums = call(
        own_kernel, "own_part", [vmem()] * 4,
        growing() + [shape(8, CORE, dtype=F32), shape(16, 128, dtype=F32)],
        flops=2 * ROWS * CORE * CORE,
    )(states, *prepared)
    return grown, state_mean, sums


def before_part(before, grown, sums, prepared):
    *grown, strip, sums = call(
        before_kernel, "before_part", [vmem()] * 11,
        growing() + [shape(RIM, ROWS), shape(16, 128, dtype=F32)],
        flops=2 * ROWS * RIM * (CORE + RIM), aliases={4 + k: k for k in range(7)},
    )(before, sums, *prepared[:2], *grown)
    return grown, strip, sums


def analyse(after, grown, strip, state_mean, sums, prepared):
    chain = pltpu.VMEM((SPAN, CORE + 128), BF16)
    return call(
        analyse_kernel, "analyse", [vmem()] * 13, growing() + [shape(ROWS, CORE)],
        scratch_shapes=[chain, chain, chain],
        flops=8 * SPAN * SPAN * CORE, aliases={6 + k: k for k in range(7)},
    )(after, strip, state_mean, sums, *prepared[:2], *grown)[-1]


def local(
    background_fields,
    measured_location,
    measured_datum,
    measured_error_spread,
    measured_distance_band,
    measured_tally,
    taper_weights,
):
    axes = ("member", "patch")
    groups = lax.axis_size("patch")
    sent = enter(jnp.transpose(background_fields, (1, 0, 2)))
    received = lax.all_to_all(sent, "member", split_axis=0, concat_axis=0, tiled=True)
    *prepared, pick = prepare(
        jnp.asarray(HOSTED), measured_tally, taper_weights, measured_location, measured_datum,
        measured_error_spread, measured_distance_band,
    )
    states = received.reshape(ROWS, CORE)
    rightward, leftward = extract(states, pick)
    owners = [CYCLES[g % 2][p] * groups + g for g in range(groups) for p in range(GROUP)]
    up = list(zip(owners, owners[1:] + owners[:1]))
    down = [(j, i) for i, j in up]
    before = lax.ppermute(rightward, axes, up)
    after = lax.ppermute(leftward, axes, down)
    grown, state_mean, sums = own_part(states, prepared)
    grown, strip, sums = before_part(before, grown, sums, prepared)
    analysed = analyse(after, grown, strip, state_mean, sums, prepared)
    analysed = analysed.reshape(GROUP, PADDED, CORE)
    returned = lax.all_to_all(analysed, "member", split_axis=0, concat_axis=0, tiled=True)
    return jnp.transpose(leave(returned), (1, 0, 2))


def solution(mesh):
    placed = (
        P("patch", "member", None),
        P("patch", None),
        P("patch", None),
        P("patch", None),
        P("patch", None),
        P("patch"),
        P(),
    )
    return jax.shard_map(
        local, mesh=mesh, in_specs=placed, out_specs=P("patch", "member", None), check_vma=False
    )
```

```python
import jax
import jax.numpy as jnp
import numpy as np
from jax import lax
from jax.experimental import pallas as pl
from jax.experimental.pallas import tpu as pltpu
from jax.sharding import PartitionSpec as P

STRATUM_PAIRS = 24
PIECE_WIDTH = 16
FRINGE_REACH = 8
NCLASS = 16
CORE = STRATUM_PAIRS * PIECE_WIDTH
RIM = STRATUM_PAIRS * FRINGE_REACH
SPAN = CORE + 2 * RIM
OBS = 640
GROUP = 32
HELD = 30
PADDED = 32
ROWS = GROUP * PADDED
MEMBERS = GROUP * HELD
EIGHT = 8
TILE = 256

F32 = jnp.float32
BF16 = jnp.bfloat16
I32 = jnp.int32

CYCLES = (
    (0, 8, 9, 17, 16, 23, 22, 14, 15, 7, 6, 5, 13, 21, 20, 12,
     4, 3, 2, 1, 25, 26, 18, 10, 11, 19, 27, 28, 29, 30, 31, 24),
    (0, 1, 9, 10, 2, 26, 27, 3, 11, 12, 13, 14, 6, 30, 22, 21,
     29, 5, 4, 28, 20, 19, 18, 17, 25, 24, 16, 8, 15, 23, 31, 7),
)
HOSTED = np.argsort(np.array(CYCLES, np.int32), axis=1).astype(np.int32).reshape(-1)


def vmem():
    return pl.BlockSpec(memory_space=pltpu.VMEM)


def smem():
    return pl.BlockSpec(memory_space=pltpu.SMEM)


def hbm():
    return pl.BlockSpec(memory_space=pltpu.HBM)


def params():
    return pltpu.CompilerParams(vmem_limit_bytes=40 * 1024 * 1024)


def shape(*dims, dtype=BF16):
    return jax.ShapeDtypeStruct(dims, dtype)


def mm(a, b):
    return jnp.dot(a, b, preferred_element_type=F32)


def mm_nt(a, b):
    return lax.dot_general(a, b, (((1,), (1,)), ((), ())), preferred_element_type=F32)


def swap_matrix(inner):
    size = GROUP * EIGHT
    row = lax.broadcasted_iota(I32, (size, size), 0)
    column = lax.broadcasted_iota(I32, (size, size), 1)
    wanted = (row & (inner - 1)) * (size // inner) + row // inner
    return jnp.where(column == wanted, 1.0, 0.0).astype(BF16)


def core_index():
    return lax.axis_index("patch") % 2


def home_of(core, patch):
    return jnp.where(core == 0, CYCLES[0][patch], CYCLES[1][patch])


def entry_kernel(states, out):
    swap = swap_matrix(EIGHT)
    core = core_index()
    for start in range(0, HELD, 2 * EIGHT):
        halves = []
        for first in (start, start + EIGHT):
            count = min(EIGHT, HELD - first)
            block = states[first : first + count].reshape(count * GROUP, CORE)
            halves.append(mm(swap[:, : count * GROUP], block))
        for p in range(GROUP):
            rows = slice(p * EIGHT, (p + 1) * EIGHT)
            both = jnp.concatenate([half[rows, :] for half in halves], axis=0)
            out[home_of(core, p), start : start + 2 * EIGHT, :] = both.astype(BF16)


def exit_kernel(analysed, out, buffer, sent):
    swap = swap_matrix(GROUP)
    core = core_index()
    copies = []
    for start in range(0, HELD, 2 * EIGHT):
        tiles = [
            analysed[home_of(core, p), start : start + 2 * EIGHT, :].astype(F32)
            for p in range(GROUP)
        ]
        for k in range(2):
            first = start + k * EIGHT
            count = min(EIGHT, HELD - first)
            block = jnp.concatenate([tile[k * EIGHT : (k + 1) * EIGHT, :] for tile in tiles], axis=0)
            moved = mm(swap[: count * GROUP, :], block.astype(BF16)).astype(BF16)
            buffer[first : first + count] = moved.reshape(count, GROUP, CORE)
        rows = slice(start, min(start + 2 * EIGHT, HELD))
        copies.append(
            pltpu.make_async_copy(buffer.at[rows], out.at[rows], sent.at[start // (2 * EIGHT)])
        )
        copies[-1].start()
    for copy in copies:
        copy.wait()


def prepare_kernel(
    hosted, tally, taper, location, datum, error_spread, band,
    root_column, ratio_column, root_row, pick,
):
    me = hosted[core_index() * GROUP + lax.axis_index("member")]
    mine = pl.ds(me, 1)
    flat = location[mine, :]
    level = flat >> 5
    column = flat & 31
    spot = level * PIECE_WIDTH + column - FRINGE_REACH
    rim = level * FRINGE_REACH + (column & (FRINGE_REACH - 1))
    spot = jnp.where(column < FRINGE_REACH, CORE + rim, spot)
    spot = jnp.where(column >= FRINGE_REACH + PIECE_WIDTH, CORE + RIM + rim, spot)

    classes = band[mine, :]
    weight = jnp.zeros(classes.shape, I32)
    for k in range(NCLASS):
        weight = jnp.where(classes == k, taper[k], weight)
    slot = lax.broadcasted_iota(I32, classes.shape, 1)
    live = jnp.where(slot < tally[me], 1.0, 0.0)
    precision = live * (weight.astype(F32) / 64.0) / error_spread[mine, :]
    pulled = precision * datum[mine, :]
    for t in range(0, SPAN, 128):
        hit = lax.broadcasted_iota(I32, (128, OBS), 0) + t == spot
        total = jnp.sum(jnp.where(hit, precision, 0.0), axis=1, keepdims=True)
        pull = jnp.sum(jnp.where(hit, pulled, 0.0), axis=1, keepdims=True)
        total = jnp.broadcast_to(total, (128, 128))
        pull = jnp.broadcast_to(pull, (128, 128))
        root = jnp.sqrt(total)
        root_column[t : t + 128, :] = root
        ratio_column[t : t + 128, :] = jnp.where(
            total > 0.0, pull / jnp.where(total > 0.0, root, 1.0), 0.0
        )
        root_row[:, t : t + 128] = root.T[0:8, :]

    row = lax.broadcasted_iota(I32, (2 * RIM, CORE), 0)
    lane = lax.broadcasted_iota(I32, (2 * RIM, CORE), 1)
    rim = jnp.where(row < RIM, row, row - RIM)
    source = (rim >> 3) * PIECE_WIDTH + (rim & (FRINGE_REACH - 1))
    source = jnp.where(row < RIM, source + PIECE_WIDTH - FRINGE_REACH, source)
    pick[...] = jnp.where(lane == source, 1.0, 0.0).astype(BF16)


def extract_kernel(states, pick, rightward, leftward):
    for t in range(0, ROWS, TILE):
        rims = mm_nt(pick[...], states[t : t + TILE, :]).astype(BF16)
        rightward[:, t : t + TILE] = rims[:RIM, :]
        leftward[:, t : t + TILE] = rims[RIM:, :]


def corners(block):
    same = lax.broadcasted_iota(I32, block.shape, 0) == lax.broadcasted_iota(I32, block.shape, 1)
    return jnp.sum(jnp.where(same, block, 0.0), keepdims=True)


def squared(block):
    return jnp.sum(block * block, keepdims=True)


def scales(peak):
    exponent = jnp.floor(jnp.log2(jnp.where(peak > 0.0, peak, 1.0)))
    exponent = jnp.minimum(jnp.maximum(exponent, -100.0), 120.0)
    return jnp.exp2(exponent), jnp.exp2(-exponent)


def own_kernel(
    states, root_column, ratio_column, root_row,
    window, gram, basis, first, pulls, weight_column, weight_row, state_mean, sums,
):
    total = jnp.zeros((1, CORE), F32)
    for t in range(0, ROWS, TILE):
        total += jnp.sum(states[t : t + TILE, :].astype(F32), axis=0, keepdims=True)
    mean = total / MEMBERS
    live = (lax.broadcasted_iota(I32, (TILE, CORE), 0) & (PADDED - 1)) < HELD
    peak = jnp.zeros((1, CORE), F32)
    for t in range(0, ROWS, TILE):
        tile = jnp.where(live, states[t : t + TILE, :].astype(F32) - mean, 0.0)
        peak = jnp.maximum(peak, jnp.max(jnp.abs(tile), axis=0, keepdims=True))
    scale, inverse = scales(peak)
    state_mean[0:1, :] = mean
    state_mean[1:2, :] = scale
    covariance = jnp.zeros((CORE, CORE), F32)
    for t in range(0, ROWS, TILE):
        tile = jnp.where(live, (states[t : t + TILE, :].astype(F32) - mean) * inverse, 0.0)
        window[t : t + TILE, :CORE] = tile.astype(BF16)
        covariance += mm(tile.T.astype(BF16), tile.astype(BF16))
    root = root_column[:CORE, :]
    weight = root * jnp.broadcast_to(scale, (128, CORE)).T
    weight_column[:CORE, :] = weight
    weight_column[CORE:, :] = root_column[CORE:, :]
    across = root_row[0:1, :CORE] * scale
    weight_row[0:1, :CORE] = across
    weight_row[0:1, CORE:] = root_row[0:1, CORE:]
    lifted = jnp.tile(weight, (1, CORE // 128)) * covariance
    basis[:CORE, :] = lifted
    first[:CORE, :CORE] = lifted.astype(BF16)
    block = lifted * across
    gram[:CORE, :CORE] = block.astype(BF16)
    pull = ratio_column[:CORE, :] - root * jnp.broadcast_to(mean, (128, CORE)).T
    pulls[:CORE, :] = pull
    first[:CORE, CORE:] = pull.astype(BF16)
    sums[0:8, :] = jnp.broadcast_to(squared(block), (8, 128))
    sums[8:16, :] = jnp.broadcast_to(corners(block), (8, 128))


def add_rim(
    rims, top, earlier, ratio_column,
    window, gram, basis, first, pulls, weight_column, weight_row,
):
    span = slice(top, top + RIM)
    live = (lax.broadcasted_iota(I32, (RIM, ROWS), 1) & (PADDED - 1)) < HELD
    tile = rims[...].astype(F32)
    mean = jnp.sum(tile, axis=1, keepdims=True) / MEMBERS
    weight = weight_column[span, :]
    seen = jnp.where(weight[:, 0:1] > 0.0, 1.0, 0.0)
    strip = jnp.where(live, (tile - mean) * seen, 0.0).astype(BF16)
    pull = ratio_column[span, :] - weight * mean
    pulls[span, :] = pull
    first[span, CORE:] = pull.astype(BF16)
    lifted = jnp.tile(weight, (1, CORE // 128)) * mm(strip, window[:, :CORE])
    basis[span, :] = lifted
    first[span, :CORE] = lifted.astype(BF16)
    block = lifted * weight_row[0:1, :CORE]
    gram[span, :CORE] = block.astype(BF16)
    gram[:CORE, span] = block.astype(BF16).T
    squares = 2.0 * squared(block)
    weight = weight[:, 0:1]
    if earlier is not None:
        block = weight * mm_nt(strip, earlier[...]) * weight_row[0:1, CORE : CORE + RIM]
        gram[span, CORE : CORE + RIM] = block.astype(BF16)
        gram[CORE : CORE + RIM, span] = block.astype(BF16).T
        squares += 2.0 * squared(block)
    block = weight * mm_nt(strip, strip) * weight_row[0:1, span]
    gram[span, span] = block.astype(BF16)
    return strip, squares + squared(block), corners(block)


def before_kernel(
    before, own_sums, ratio_column,
    _window, _gram, _basis, _first, _pulls, _weight_column, _weight_row,
    window, gram, basis, first, pulls, weight_column, weight_row, strip, sums,
):
    added, squares, trace = add_rim(
        before, CORE, None, ratio_column,
        window, gram, basis, first, pulls, weight_column, weight_row,
    )
    strip[...] = added
    window[:, CORE : CORE + RIM] = added.T
    sums[0:8, :] = own_sums[0:8, :] + squares
    sums[8:16, :] = own_sums[8:16, :] + trace


def analyse_kernel(
    after, strip, state_mean, sums, ratio_column,
    _window, _gram, _basis, _first, _pulls, _weight_column, _weight_row,
    window, gram, basis, first, pulls, weight_column, weight_row, out, second, third, fourth,
):
    added, squares, trace = add_rim(
        after, CORE + RIM, strip, ratio_column,
        window, gram, basis, first, pulls, weight_column, weight_row,
    )
    squares += sums[0:1, 0:1]
    trace += sums[8:9, 0:1]
    draw = F32(MEMBERS - 1)
    inverse = 1.0 / (draw + 2.0 * squares / (draw + trace))

    a = draw * inverse
    r = 1.5 - 0.5 * a
    s = 1.5 - 0.5 * a * r * r
    halves = ((slice(0, 256), slice(0, 256)), (slice(256, CORE), slice(0, 128)))
    last = slice(CORE, CORE + 128)

    def product(source, h):
        return mm(gram[...], source[:, h * 256 : (h + 1) * 256])

    def one(h, p):
        wide, part = halves[h]
        v = (0.25 * inverse * inverse) * p[:, part] - (r * inverse) * basis[:, wide]
        second[:, wide] = v.astype(BF16)
        if h:
            second[:, last] = (r * pulls[...] - (0.5 * inverse) * p[:, 128:]).astype(BF16)

    def two(h, p):
        wide, part = halves[h]
        v = (-0.5 * a) * second[:, wide].astype(F32) - (0.5 * inverse) * p[:, part]
        v -= (0.5 * r * r * inverse) * basis[:, wide]
        third[:, wide] = v.astype(BF16)
        if h:
            x = r * second[:, last].astype(F32) - (0.5 * inverse) * p[:, 128:]
            third[:, last] = x.astype(BF16)

    def three(h, p):
        wide, part = halves[h]
        v = r * third[:, wide].astype(F32) - (0.5 * inverse) * p[:, part]
        v -= (0.5 * s * inverse) * basis[:, wide]
        fourth[:, wide] = v.astype(BF16)
        first[:, wide] = (jnp.tile(weight_column[...], (1, v.shape[1] // 128)) * v).astype(BF16)
        if h:
            x = (-0.5 * a) * third[:, last].astype(F32) - (0.5 * inverse) * p[:, 128:]
            fourth[:, last] = (1.5 * pulls[...] + x).astype(BF16)

    chain = (first, second, third, fourth)
    waiting = [product(first, 0), product(first, 1)]
    window[:, CORE + RIM :] = added.T
    for k, finish in enumerate((one, two, three)):
        for h in range(2):
            finish(h, waiting[h])
            waiting[h] = product(chain[k + 1], h)
    x = r * fourth[:, last].astype(F32) - (0.5 * inverse) * waiting[1][:, 128:]
    x *= inverse
    shift = []
    for h, (wide, part) in enumerate(halves):
        for t in range(part.start, part.stop, 128):
            both = (r * s) * basis[:, h * 256 + t : h * 256 + t + 128] + waiting[h][:, t : t + 128]
            shift.append(jnp.sum(x * both, axis=0, keepdims=True))
    scale = state_mean[1:2, :]
    base = state_mean[0:1, :] + scale * jnp.concatenate(shift, axis=1)
    gain = jnp.sqrt(a) * scale
    for t in range(0, ROWS, TILE):
        rows = slice(t, t + TILE)
        moved = mm(window[rows, :], first[:, :CORE])
        moved += r * s * window[rows, :CORE].astype(F32)
        out[rows, :] = (base + gain * moved).astype(BF16)


def call(
    kernel, name, in_specs, out_shape, out_specs=None, scratch_shapes=(), flops=0, aliases=None
):
    return pl.pallas_call(
        kernel,
        in_specs=in_specs,
        out_specs=out_specs or jax.tree.map(lambda _: vmem(), out_shape),
        out_shape=out_shape,
        scratch_shapes=list(scratch_shapes),
        input_output_aliases=aliases or {},
        compiler_params=params(),
        cost_estimate=pl.CostEstimate(flops=flops, bytes_accessed=1 << 20, transcendentals=0),
        name=name,
    )


def enter(states):
    return call(
        entry_kernel, "entry", [vmem()], shape(GROUP, PADDED, CORE), flops=8 * 256 * 256 * CORE
    )(states)


def leave(analysed):
    return call(
        exit_kernel, "exit", [vmem()], shape(HELD, GROUP, CORE), hbm(),
        [pltpu.VMEM((HELD, GROUP, CORE), BF16), pltpu.SemaphoreType.DMA((2,))],
        8 * 256 * 256 * CORE,
    )(analysed)


def prepare(hosted, tally, taper, location, datum, error_spread, band):
    return call(
        prepare_kernel, "prepare", [smem()] * 3 + [vmem()] * 4,
        [shape(SPAN, 128, dtype=F32), shape(SPAN, 128, dtype=F32), shape(8, SPAN, dtype=F32),
         shape(2 * RIM, CORE)],
        flops=4 * SPAN * OBS,
    )(hosted, tally, taper, location, datum, error_spread, band)


def extract(states, pick):
    return call(
        extract_kernel, "extract", [vmem()] * 2, [shape(RIM, ROWS), shape(RIM, ROWS)],
        flops=4 * RIM * CORE * ROWS,
    )(states, pick)


def growing():
    return [
        shape(ROWS, SPAN), shape(SPAN, SPAN), shape(SPAN, CORE, dtype=F32),
        shape(SPAN, CORE + 128), shape(SPAN, 128, dtype=F32),
        shape(SPAN, 128, dtype=F32), shape(8, SPAN, dtype=F32),
    ]


def own_part(states, prepared):
    *grown, state_mean, sums = call(
        own_kernel, "own_part", [vmem()] * 4,
        growing() + [shape(8, CORE, dtype=F32), shape(16, 128, dtype=F32)],
        flops=2 * ROWS * CORE * CORE,
    )(states, *prepared)
    return grown, state_mean, sums


def before_part(before, grown, sums, prepared):
    *grown, strip, sums = call(
        before_kernel, "before_part", [vmem()] * 10,
        growing() + [shape(RIM, ROWS), shape(16, 128, dtype=F32)],
        flops=2 * ROWS * RIM * (CORE + RIM), aliases={3 + k: k for k in range(7)},
    )(before, sums, prepared[1], *grown)
    return grown, strip, sums


def analyse(after, grown, strip, state_mean, sums, prepared):
    chain = pltpu.VMEM((SPAN, CORE + 128), BF16)
    return call(
        analyse_kernel, "analyse", [vmem()] * 12, growing() + [shape(ROWS, CORE)],
        scratch_shapes=[chain, chain, chain],
        flops=8 * SPAN * SPAN * CORE, aliases={5 + k: k for k in range(7)},
    )(after, strip, state_mean, sums, prepared[1], *grown)[-1]


def local(
    background_fields,
    measured_location,
    measured_datum,
    measured_error_spread,
    measured_distance_band,
    measured_tally,
    taper_weights,
):
    axes = ("member", "patch")
    groups = lax.axis_size("patch")
    sent = enter(jnp.transpose(background_fields, (1, 0, 2)))
    received = lax.all_to_all(sent, "member", split_axis=0, concat_axis=0, tiled=True)
    *prepared, pick = prepare(
        jnp.asarray(HOSTED), measured_tally, taper_weights, measured_location, measured_datum,
        measured_error_spread, measured_distance_band,
    )
    states = received.reshape(ROWS, CORE)
    rightward, leftward = extract(states, pick)
    owners = [CYCLES[g % 2][p] * groups + g for g in range(groups) for p in range(GROUP)]
    up = list(zip(owners, owners[1:] + owners[:1]))
    down = [(j, i) for i, j in up]
    before = lax.ppermute(rightward, axes, up)
    after = lax.ppermute(leftward, axes, down)
    grown, state_mean, sums = own_part(states, prepared)
    grown, strip, sums = before_part(before, grown, sums, prepared)
    analysed = analyse(after, grown, strip, state_mean, sums, prepared)
    analysed = analysed.reshape(GROUP, PADDED, CORE)
    returned = lax.all_to_all(analysed, "member", split_axis=0, concat_axis=0, tiled=True)
    return jnp.transpose(leave(returned), (1, 0, 2))


def solution(mesh):
    placed = (
        P("patch", "member", None),
        P("patch", None),
        P("patch", None),
        P("patch", None),
        P("patch", None),
        P("patch"),
        P(),
    )
    return jax.shard_map(
        local, mesh=mesh, in_specs=placed, out_specs=P("patch", "member", None), check_vma=False
    )
```

```python
import jax
import jax.numpy as jnp
import numpy as np
from jax import lax
from jax.experimental import pallas as pl
from jax.experimental.pallas import tpu as pltpu
from jax.sharding import PartitionSpec as P

STRATUM_PAIRS = 24
PIECE_WIDTH = 16
FRINGE_REACH = 8
NCLASS = 16
CORE = STRATUM_PAIRS * PIECE_WIDTH
RIM = STRATUM_PAIRS * FRINGE_REACH
SPAN = CORE + 2 * RIM
OBS = 640
GROUP = 32
HELD = 30
PADDED = 32
ROWS = GROUP * PADDED
MEMBERS = GROUP * HELD
EIGHT = 8
TILE = 256

F32 = jnp.float32
BF16 = jnp.bfloat16
I32 = jnp.int32

CYCLES = (
    (0, 8, 9, 17, 16, 23, 22, 14, 15, 7, 6, 5, 13, 21, 20, 12,
     4, 3, 2, 1, 25, 26, 18, 10, 11, 19, 27, 28, 29, 30, 31, 24),
    (0, 1, 9, 10, 2, 26, 27, 3, 11, 12, 13, 14, 6, 30, 22, 21,
     29, 5, 4, 28, 20, 19, 18, 17, 25, 24, 16, 8, 15, 23, 31, 7),
)
HOSTED = np.argsort(np.array(CYCLES, np.int32), axis=1).astype(np.int32).reshape(-1)


def vmem():
    return pl.BlockSpec(memory_space=pltpu.VMEM)


def smem():
    return pl.BlockSpec(memory_space=pltpu.SMEM)


def hbm():
    return pl.BlockSpec(memory_space=pltpu.HBM)


def params():
    return pltpu.CompilerParams(vmem_limit_bytes=40 * 1024 * 1024)


def shape(*dims, dtype=BF16):
    return jax.ShapeDtypeStruct(dims, dtype)


def mm(a, b):
    return jnp.dot(a, b, preferred_element_type=F32)


def mm_nt(a, b):
    return lax.dot_general(a, b, (((1,), (1,)), ((), ())), preferred_element_type=F32)


def swap_matrix(inner):
    size = GROUP * EIGHT
    row = lax.broadcasted_iota(I32, (size, size), 0)
    column = lax.broadcasted_iota(I32, (size, size), 1)
    wanted = (row & (inner - 1)) * (size // inner) + row // inner
    return jnp.where(column == wanted, 1.0, 0.0).astype(BF16)


def core_index():
    return lax.axis_index("patch") % 2


def home_of(core, patch):
    return jnp.where(core == 0, CYCLES[0][patch], CYCLES[1][patch])


def entry_kernel(states, out):
    swap = swap_matrix(EIGHT)
    core = core_index()
    for start in range(0, HELD, 2 * EIGHT):
        halves = []
        for first in (start, start + EIGHT):
            count = min(EIGHT, HELD - first)
            block = states[first : first + count].reshape(count * GROUP, CORE)
            halves.append(mm(swap[:, : count * GROUP], block))
        for p in range(GROUP):
            rows = slice(p * EIGHT, (p + 1) * EIGHT)
            both = jnp.concatenate([half[rows, :] for half in halves], axis=0)
            out[home_of(core, p), start : start + 2 * EIGHT, :] = both.astype(BF16)


def exit_kernel(analysed, out, buffer, sent):
    swap = swap_matrix(GROUP)
    core = core_index()
    copies = []
    for start in range(0, HELD, 2 * EIGHT):
        tiles = [
            analysed[home_of(core, p), start : start + 2 * EIGHT, :].astype(F32)
            for p in range(GROUP)
        ]
        for k in range(2):
            first = start + k * EIGHT
            count = min(EIGHT, HELD - first)
            block = jnp.concatenate([tile[k * EIGHT : (k + 1) * EIGHT, :] for tile in tiles], axis=0)
            moved = mm(swap[: count * GROUP, :], block.astype(BF16)).astype(BF16)
            rows = slice(first, first + count)
            buffer[rows] = moved.reshape(count, GROUP, CORE)
            copies.append(
                pltpu.make_async_copy(buffer.at[rows], out.at[rows], sent.at[first // EIGHT])
            )
            copies[-1].start()
    for copy in copies:
        copy.wait()


def prepare_kernel(
    hosted, tally, taper, location, datum, error_spread, band,
    root_column, ratio_column, root_row, pick,
):
    me = hosted[core_index() * GROUP + lax.axis_index("member")]
    mine = pl.ds(me, 1)
    flat = location[mine, :]
    level = flat >> 5
    column = flat & 31
    spot = level * PIECE_WIDTH + column - FRINGE_REACH
    rim = level * FRINGE_REACH + (column & (FRINGE_REACH - 1))
    spot = jnp.where(column < FRINGE_REACH, CORE + rim, spot)
    spot = jnp.where(column >= FRINGE_REACH + PIECE_WIDTH, CORE + RIM + rim, spot)

    classes = band[mine, :]
    weight = jnp.zeros(classes.shape, I32)
    for k in range(NCLASS):
        weight = jnp.where(classes == k, taper[k], weight)
    slot = lax.broadcasted_iota(I32, classes.shape, 1)
    live = jnp.where(slot < tally[me], 1.0, 0.0)
    precision = live * (weight.astype(F32) / 64.0) / error_spread[mine, :]
    pulled = precision * datum[mine, :]
    for t in range(0, SPAN, 128):
        hit = lax.broadcasted_iota(I32, (128, OBS), 0) + t == spot
        total = jnp.sum(jnp.where(hit, precision, 0.0), axis=1, keepdims=True)
        pull = jnp.sum(jnp.where(hit, pulled, 0.0), axis=1, keepdims=True)
        total = jnp.broadcast_to(total, (128, 128))
        pull = jnp.broadcast_to(pull, (128, 128))
        root = jnp.sqrt(total)
        root_column[t : t + 128, :] = root
        ratio_column[t : t + 128, :] = jnp.where(
            total > 0.0, pull / jnp.where(total > 0.0, root, 1.0), 0.0
        )
        root_row[:, t : t + 128] = root.T[0:8, :]

    row = lax.broadcasted_iota(I32, (2 * RIM, CORE), 0)
    lane = lax.broadcasted_iota(I32, (2 * RIM, CORE), 1)
    rim = jnp.where(row < RIM, row, row - RIM)
    source = (rim >> 3) * PIECE_WIDTH + (rim & (FRINGE_REACH - 1))
    source = jnp.where(row < RIM, source + PIECE_WIDTH - FRINGE_REACH, source)
    pick[...] = jnp.where(lane == source, 1.0, 0.0).astype(BF16)


def extract_kernel(states, pick, rightward, leftward):
    for t in range(0, ROWS, TILE):
        rims = mm_nt(pick[...], states[t : t + TILE, :]).astype(BF16)
        rightward[:, t : t + TILE] = rims[:RIM, :]
        leftward[:, t : t + TILE] = rims[RIM:, :]


def corners(block):
    same = lax.broadcasted_iota(I32, block.shape, 0) == lax.broadcasted_iota(I32, block.shape, 1)
    return jnp.sum(jnp.where(same, block, 0.0), keepdims=True)


def squared(block):
    return jnp.sum(block * block, keepdims=True)


def scales(peak):
    exponent = jnp.floor(jnp.log2(jnp.where(peak > 0.0, peak, 1.0)))
    exponent = jnp.minimum(jnp.maximum(exponent, -100.0), 120.0)
    return jnp.exp2(exponent), jnp.exp2(-exponent)


def own_kernel(
    states, root_column, ratio_column, root_row,
    window, gram, basis, first, pulls, weight_column, weight_row, state_mean, sums,
):
    total = jnp.zeros((1, CORE), F32)
    for t in range(0, ROWS, TILE):
        total += jnp.sum(states[t : t + TILE, :].astype(F32), axis=0, keepdims=True)
    mean = total / MEMBERS
    live = (lax.broadcasted_iota(I32, (TILE, CORE), 0) & (PADDED - 1)) < HELD
    peak = jnp.zeros((1, CORE), F32)
    for t in range(0, ROWS, TILE):
        tile = jnp.where(live, states[t : t + TILE, :].astype(F32) - mean, 0.0)
        peak = jnp.maximum(peak, jnp.max(jnp.abs(tile), axis=0, keepdims=True))
    scale, inverse = scales(peak)
    state_mean[0:1, :] = mean
    state_mean[1:2, :] = scale
    covariance = jnp.zeros((CORE, CORE), F32)
    for t in range(0, ROWS, TILE):
        tile = jnp.where(live, (states[t : t + TILE, :].astype(F32) - mean) * inverse, 0.0)
        window[t : t + TILE, :CORE] = tile.astype(BF16)
        covariance += mm(tile.T.astype(BF16), tile.astype(BF16))
    root = root_column[:CORE, :]
    weight = root * jnp.broadcast_to(scale, (128, CORE)).T
    weight_column[:CORE, :] = weight
    weight_column[CORE:, :] = root_column[CORE:, :]
    across = root_row[0:1, :CORE] * scale
    weight_row[0:1, :CORE] = across
    weight_row[0:1, CORE:] = root_row[0:1, CORE:]
    lifted = jnp.tile(weight, (1, CORE // 128)) * covariance
    basis[:CORE, :] = lifted
    first[:CORE, :CORE] = lifted.astype(BF16)
    block = lifted * across
    gram[:CORE, :CORE] = block.astype(BF16)
    pull = ratio_column[:CORE, :] - root * jnp.broadcast_to(mean, (128, CORE)).T
    pulls[:CORE, :] = pull
    first[:CORE, CORE:] = pull.astype(BF16)
    sums[0:8, :] = jnp.broadcast_to(squared(block), (8, 128))
    sums[8:16, :] = jnp.broadcast_to(corners(block), (8, 128))


def add_rim(
    rims, top, earlier, ratio_column,
    window, gram, basis, first, pulls, weight_column, weight_row,
):
    span = slice(top, top + RIM)
    live = (lax.broadcasted_iota(I32, (RIM, ROWS), 1) & (PADDED - 1)) < HELD
    tile = rims[...].astype(F32)
    mean = jnp.sum(tile, axis=1, keepdims=True) / MEMBERS
    weight = weight_column[span, :]
    seen = jnp.where(weight[:, 0:1] > 0.0, 1.0, 0.0)
    strip = jnp.where(live, (tile - mean) * seen, 0.0).astype(BF16)
    pull = ratio_column[span, :] - weight * mean
    pulls[span, :] = pull
    first[span, CORE:] = pull.astype(BF16)
    lifted = jnp.tile(weight, (1, CORE // 128)) * mm(strip, window[:, :CORE])
    basis[span, :] = lifted
    first[span, :CORE] = lifted.astype(BF16)
    block = lifted * weight_row[0:1, :CORE]
    gram[span, :CORE] = block.astype(BF16)
    gram[:CORE, span] = block.astype(BF16).T
    squares = 2.0 * squared(block)
    weight = weight[:, 0:1]
    if earlier is not None:
        block = weight * mm_nt(strip, earlier[...]) * weight_row[0:1, CORE : CORE + RIM]
        gram[span, CORE : CORE + RIM] = block.astype(BF16)
        gram[CORE : CORE + RIM, span] = block.astype(BF16).T
        squares += 2.0 * squared(block)
    block = weight * mm_nt(strip, strip) * weight_row[0:1, span]
    gram[span, span] = block.astype(BF16)
    return strip, squares + squared(block), corners(block)


def before_kernel(
    before, own_sums, ratio_column,
    _window, _gram, _basis, _first, _pulls, _weight_column, _weight_row,
    window, gram, basis, first, pulls, weight_column, weight_row, strip, sums,
):
    added, squares, trace = add_rim(
        before, CORE, None, ratio_column,
        window, gram, basis, first, pulls, weight_column, weight_row,
    )
    strip[...] = added
    window[:, CORE : CORE + RIM] = added.T
    sums[0:8, :] = own_sums[0:8, :] + squares
    sums[8:16, :] = own_sums[8:16, :] + trace


def analyse_kernel(
    after, strip, state_mean, sums, ratio_column,
    _window, _gram, _basis, _first, _pulls, _weight_column, _weight_row,
    window, gram, basis, first, pulls, weight_column, weight_row, out, second, third, fourth,
):
    added, squares, trace = add_rim(
        after, CORE + RIM, strip, ratio_column,
        window, gram, basis, first, pulls, weight_column, weight_row,
    )
    squares += sums[0:1, 0:1]
    trace += sums[8:9, 0:1]
    draw = F32(MEMBERS - 1)
    inverse = 1.0 / (draw + 2.0 * squares / (draw + trace))

    a = draw * inverse
    r = 1.5 - 0.5 * a
    s = 1.5 - 0.5 * a * r * r
    halves = ((slice(0, 256), slice(0, 256)), (slice(256, CORE), slice(0, 128)))
    last = slice(CORE, CORE + 128)

    def product(source, h):
        return mm(gram[...], source[:, h * 256 : (h + 1) * 256])

    def one(h, p):
        wide, part = halves[h]
        v = (0.25 * inverse * inverse) * p[:, part] - (r * inverse) * basis[:, wide]
        second[:, wide] = v.astype(BF16)
        if h:
            second[:, last] = (r * pulls[...] - (0.5 * inverse) * p[:, 128:]).astype(BF16)

    def two(h, p):
        wide, part = halves[h]
        v = (-0.5 * a) * second[:, wide].astype(F32) - (0.5 * inverse) * p[:, part]
        v -= (0.5 * r * r * inverse) * basis[:, wide]
        third[:, wide] = v.astype(BF16)
        if h:
            x = r * second[:, last].astype(F32) - (0.5 * inverse) * p[:, 128:]
            third[:, last] = x.astype(BF16)

    def three(h, p):
        wide, part = halves[h]
        v = r * third[:, wide].astype(F32) - (0.5 * inverse) * p[:, part]
        v -= (0.5 * s * inverse) * basis[:, wide]
        fourth[:, wide] = v.astype(BF16)
        first[:, wide] = (jnp.tile(weight_column[...], (1, v.shape[1] // 128)) * v).astype(BF16)
        if h:
            x = (-0.5 * a) * third[:, last].astype(F32) - (0.5 * inverse) * p[:, 128:]
            fourth[:, last] = (1.5 * pulls[...] + x).astype(BF16)

    chain = (first, second, third, fourth)
    waiting = [product(first, 0), product(first, 1)]
    window[:, CORE + RIM :] = added.T
    for k, finish in enumerate((one, two, three)):
        for h in range(2):
            finish(h, waiting[h])
            waiting[h] = product(chain[k + 1], h)
    x = r * fourth[:, last].astype(F32) - (0.5 * inverse) * waiting[1][:, 128:]
    x *= inverse
    shift = []
    for h, (wide, part) in enumerate(halves):
        for t in range(part.start, part.stop, 128):
            both = (r * s) * basis[:, h * 256 + t : h * 256 + t + 128] + waiting[h][:, t : t + 128]
            shift.append(jnp.sum(x * both, axis=0, keepdims=True))
    scale = state_mean[1:2, :]
    base = state_mean[0:1, :] + scale * jnp.concatenate(shift, axis=1)
    gain = jnp.sqrt(a) * scale
    for t in range(0, ROWS, TILE):
        rows = slice(t, t + TILE)
        moved = mm(window[rows, :], first[:, :CORE])
        moved += r * s * window[rows, :CORE].astype(F32)
        out[rows, :] = (base + gain * moved).astype(BF16)


def call(
    kernel, name, in_specs, out_shape, out_specs=None, scratch_shapes=(), flops=0, aliases=None
):
    return pl.pallas_call(
        kernel,
        in_specs=in_specs,
        out_specs=out_specs or jax.tree.map(lambda _: vmem(), out_shape),
        out_shape=out_shape,
        scratch_shapes=list(scratch_shapes),
        input_output_aliases=aliases or {},
        compiler_params=params(),
        cost_estimate=pl.CostEstimate(flops=flops, bytes_accessed=1 << 20, transcendentals=0),
        name=name,
    )


def enter(states):
    return call(
        entry_kernel, "entry", [vmem()], shape(GROUP, PADDED, CORE), flops=8 * 256 * 256 * CORE
    )(states)


def leave(analysed):
    return call(
        exit_kernel, "exit", [vmem()], shape(HELD, GROUP, CORE), hbm(),
        [pltpu.VMEM((HELD, GROUP, CORE), BF16), pltpu.SemaphoreType.DMA((4,))],
        8 * 256 * 256 * CORE,
    )(analysed)


def prepare(hosted, tally, taper, location, datum, error_spread, band):
    return call(
        prepare_kernel, "prepare", [smem()] * 3 + [vmem()] * 4,
        [shape(SPAN, 128, dtype=F32), shape(SPAN, 128, dtype=F32), shape(8, SPAN, dtype=F32),
         shape(2 * RIM, CORE)],
        flops=4 * SPAN * OBS,
    )(hosted, tally, taper, location, datum, error_spread, band)


def extract(states, pick):
    return call(
        extract_kernel, "extract", [vmem()] * 2, [shape(RIM, ROWS), shape(RIM, ROWS)],
        flops=4 * RIM * CORE * ROWS,
    )(states, pick)


def growing():
    return [
        shape(ROWS, SPAN), shape(SPAN, SPAN), shape(SPAN, CORE, dtype=F32),
        shape(SPAN, CORE + 128), shape(SPAN, 128, dtype=F32),
        shape(SPAN, 128, dtype=F32), shape(8, SPAN, dtype=F32),
    ]


def own_part(states, prepared):
    *grown, state_mean, sums = call(
        own_kernel, "own_part", [vmem()] * 4,
        growing() + [shape(8, CORE, dtype=F32), shape(16, 128, dtype=F32)],
        flops=2 * ROWS * CORE * CORE,
    )(states, *prepared)
    return grown, state_mean, sums


def before_part(before, grown, sums, prepared):
    *grown, strip, sums = call(
        before_kernel, "before_part", [vmem()] * 10,
        growing() + [shape(RIM, ROWS), shape(16, 128, dtype=F32)],
        flops=2 * ROWS * RIM * (CORE + RIM), aliases={3 + k: k for k in range(7)},
    )(before, sums, prepared[1], *grown)
    return grown, strip, sums


def analyse(after, grown, strip, state_mean, sums, prepared):
    chain = pltpu.VMEM((SPAN, CORE + 128), BF16)
    return call(
        analyse_kernel, "analyse", [vmem()] * 12, growing() + [shape(ROWS, CORE)],
        scratch_shapes=[chain, chain, chain],
        flops=8 * SPAN * SPAN * CORE, aliases={5 + k: k for k in range(7)},
    )(after, strip, state_mean, sums, prepared[1], *grown)[-1]


def local(
    background_fields,
    measured_location,
    measured_datum,
    measured_error_spread,
    measured_distance_band,
    measured_tally,
    taper_weights,
):
    axes = ("member", "patch")
    groups = lax.axis_size("patch")
    sent = enter(jnp.transpose(background_fields, (1, 0, 2)))
    received = lax.all_to_all(sent, "member", split_axis=0, concat_axis=0, tiled=True)
    *prepared, pick = prepare(
        jnp.asarray(HOSTED), measured_tally, taper_weights, measured_location, measured_datum,
        measured_error_spread, measured_distance_band,
    )
    states = received.reshape(ROWS, CORE)
    rightward, leftward = extract(states, pick)
    owners = [CYCLES[g % 2][p] * groups + g for g in range(groups) for p in range(GROUP)]
    up = list(zip(owners, owners[1:] + owners[:1]))
    down = [(j, i) for i, j in up]
    before = lax.ppermute(rightward, axes, up)
    after = lax.ppermute(leftward, axes, down)
    grown, state_mean, sums = own_part(states, prepared)
    grown, strip, sums = before_part(before, grown, sums, prepared)
    analysed = analyse(after, grown, strip, state_mean, sums, prepared)
    analysed = analysed.reshape(GROUP, PADDED, CORE)
    returned = lax.all_to_all(analysed, "member", split_axis=0, concat_axis=0, tiled=True)
    return jnp.transpose(leave(returned), (1, 0, 2))


def solution(mesh):
    placed = (
        P("patch", "member", None),
        P("patch", None),
        P("patch", None),
        P("patch", None),
        P("patch", None),
        P("patch"),
        P(),
    )
    return jax.shard_map(
        local, mesh=mesh, in_specs=placed, out_specs=P("patch", "member", None), check_vma=False
    )
```

```python
import jax
import jax.numpy as jnp
import numpy as np
from jax import lax
from jax.experimental import pallas as pl
from jax.experimental.pallas import tpu as pltpu
from jax.sharding import PartitionSpec as P

STRATUM_PAIRS = 24
PIECE_WIDTH = 16
FRINGE_REACH = 8
NCLASS = 16
CORE = STRATUM_PAIRS * PIECE_WIDTH
RIM = STRATUM_PAIRS * FRINGE_REACH
SPAN = CORE + 2 * RIM
OBS = 640
GROUP = 32
HELD = 30
PADDED = 32
ROWS = GROUP * PADDED
MEMBERS = GROUP * HELD
EIGHT = 8
TILE = 256

F32 = jnp.float32
BF16 = jnp.bfloat16
I32 = jnp.int32

CYCLES = (
    (0, 8, 9, 17, 16, 23, 22, 14, 15, 7, 6, 5, 13, 21, 20, 12,
     4, 3, 2, 1, 25, 26, 18, 10, 11, 19, 27, 28, 29, 30, 31, 24),
    (0, 1, 9, 10, 2, 26, 27, 3, 11, 12, 13, 14, 6, 30, 22, 21,
     29, 5, 4, 28, 20, 19, 18, 17, 25, 24, 16, 8, 15, 23, 31, 7),
)
HOSTED = np.argsort(np.array(CYCLES, np.int32), axis=1).astype(np.int32).reshape(-1)


def vmem():
    return pl.BlockSpec(memory_space=pltpu.VMEM)


def smem():
    return pl.BlockSpec(memory_space=pltpu.SMEM)


def hbm():
    return pl.BlockSpec(memory_space=pltpu.HBM)


def params():
    return pltpu.CompilerParams(vmem_limit_bytes=40 * 1024 * 1024)


def shape(*dims, dtype=BF16):
    return jax.ShapeDtypeStruct(dims, dtype)


def mm(a, b):
    return jnp.dot(a, b, preferred_element_type=F32)


def mm_nt(a, b):
    return lax.dot_general(a, b, (((1,), (1,)), ((), ())), preferred_element_type=F32)


def swap_matrix(inner):
    size = GROUP * EIGHT
    row = lax.broadcasted_iota(I32, (size, size), 0)
    column = lax.broadcasted_iota(I32, (size, size), 1)
    wanted = (row & (inner - 1)) * (size // inner) + row // inner
    return jnp.where(column == wanted, 1.0, 0.0).astype(BF16)


def core_index():
    return lax.axis_index("patch") % 2


def home_of(core, patch):
    return jnp.where(core == 0, CYCLES[0][patch], CYCLES[1][patch])


def entry_kernel(states, out):
    swap = swap_matrix(EIGHT)
    core = core_index()
    for start in range(0, HELD, 2 * EIGHT):
        halves = []
        for first in (start, start + EIGHT):
            count = min(EIGHT, HELD - first)
            block = states[first : first + count].reshape(count * GROUP, CORE)
            halves.append(mm(swap[:, : count * GROUP], block))
        for p in range(GROUP):
            rows = slice(p * EIGHT, (p + 1) * EIGHT)
            both = jnp.concatenate([half[rows, :] for half in halves], axis=0)
            out[home_of(core, p), start : start + 2 * EIGHT, :] = both.astype(BF16)


def exit_kernel(analysed, out, buffer, sent):
    swap = swap_matrix(GROUP)
    core = core_index()
    copies = []
    for start in range(0, HELD, 2 * EIGHT):
        tiles = [
            analysed[home_of(core, p), start : start + 2 * EIGHT, :].astype(F32)
            for p in range(GROUP)
        ]
        for k in range(2):
            first = start + k * EIGHT
            count = min(EIGHT, HELD - first)
            block = jnp.concatenate([tile[k * EIGHT : (k + 1) * EIGHT, :] for tile in tiles], axis=0)
            moved = mm(swap[: count * GROUP, :], block.astype(BF16)).astype(BF16)
            rows = slice(first, first + count)
            buffer[rows] = moved.reshape(count, GROUP, CORE)
            copies.append(
                pltpu.make_async_copy(buffer.at[rows], out.at[rows], sent.at[first // EIGHT])
            )
            copies[-1].start()
    for copy in copies:
        copy.wait()


def prepare_kernel(
    hosted, tally, taper, location, datum, error_spread, band,
    root_column, ratio_column, root_row, pick,
):
    me = hosted[core_index() * GROUP + lax.axis_index("member")]
    mine = pl.ds(me, 1)
    flat = location[mine, :]
    level = flat >> 5
    column = flat & 31
    spot = level * PIECE_WIDTH + column - FRINGE_REACH
    rim = level * FRINGE_REACH + (column & (FRINGE_REACH - 1))
    spot = jnp.where(column < FRINGE_REACH, CORE + rim, spot)
    spot = jnp.where(column >= FRINGE_REACH + PIECE_WIDTH, CORE + RIM + rim, spot)

    classes = band[mine, :]
    weight = jnp.zeros(classes.shape, I32)
    for k in range(NCLASS):
        weight = jnp.where(classes == k, taper[k], weight)
    slot = lax.broadcasted_iota(I32, classes.shape, 1)
    live = jnp.where(slot < tally[me], 1.0, 0.0)
    precision = live * (weight.astype(F32) / 64.0) / error_spread[mine, :]
    pulled = precision * datum[mine, :]
    for t in range(0, SPAN, 128):
        hit = lax.broadcasted_iota(I32, (128, OBS), 0) + t == spot
        total = jnp.sum(jnp.where(hit, precision, 0.0), axis=1, keepdims=True)
        pull = jnp.sum(jnp.where(hit, pulled, 0.0), axis=1, keepdims=True)
        total = jnp.broadcast_to(total, (128, 128))
        pull = jnp.broadcast_to(pull, (128, 128))
        root = jnp.sqrt(total)
        root_column[t : t + 128, :] = root
        ratio_column[t : t + 128, :] = jnp.where(
            total > 0.0, pull / jnp.where(total > 0.0, root, 1.0), 0.0
        )
        root_row[:, t : t + 128] = root.T[0:8, :]

    row = lax.broadcasted_iota(I32, (2 * RIM, CORE), 0)
    lane = lax.broadcasted_iota(I32, (2 * RIM, CORE), 1)
    rim = jnp.where(row < RIM, row, row - RIM)
    source = (rim >> 3) * PIECE_WIDTH + (rim & (FRINGE_REACH - 1))
    source = jnp.where(row < RIM, source + PIECE_WIDTH - FRINGE_REACH, source)
    pick[...] = jnp.where(lane == source, 1.0, 0.0).astype(BF16)


def extract_kernel(states, pick, rightward, leftward):
    for t in range(0, ROWS, TILE):
        rims = mm_nt(pick[...], states[t : t + TILE, :]).astype(BF16)
        rightward[:, t : t + TILE] = rims[:RIM, :]
        leftward[:, t : t + TILE] = rims[RIM:, :]


def corners(block):
    same = lax.broadcasted_iota(I32, block.shape, 0) == lax.broadcasted_iota(I32, block.shape, 1)
    return jnp.sum(jnp.where(same, block, 0.0), keepdims=True)


def squared(block):
    return jnp.sum(block * block, keepdims=True)


def scales(peak):
    exponent = jnp.floor(jnp.log2(jnp.where(peak > 0.0, peak, 1.0)))
    exponent = jnp.minimum(jnp.maximum(exponent, -100.0), 120.0)
    return jnp.exp2(exponent), jnp.exp2(-exponent)


def own_kernel(
    states, root_column, ratio_column, root_row,
    window, gram, basis, first, pulls, weight_column, weight_row, state_mean, sums,
):
    total = jnp.zeros((1, CORE), F32)
    for t in range(0, ROWS, TILE):
        total += jnp.sum(states[t : t + TILE, :].astype(F32), axis=0, keepdims=True)
    mean = total / MEMBERS
    live = (lax.broadcasted_iota(I32, (TILE, CORE), 0) & (PADDED - 1)) < HELD
    peak = jnp.zeros((1, CORE), F32)
    for t in range(0, ROWS, TILE):
        tile = jnp.where(live, states[t : t + TILE, :].astype(F32) - mean, 0.0)
        peak = jnp.maximum(peak, jnp.max(jnp.abs(tile), axis=0, keepdims=True))
    scale, inverse = scales(peak)
    state_mean[0:1, :] = mean
    state_mean[1:2, :] = scale
    covariance = jnp.zeros((CORE, CORE), F32)
    for t in range(0, ROWS, TILE):
        tile = jnp.where(live, (states[t : t + TILE, :].astype(F32) - mean) * inverse, 0.0)
        window[t : t + TILE, :CORE] = tile.astype(BF16)
        covariance += mm(tile.T.astype(BF16), tile.astype(BF16))
    root = root_column[:CORE, :]
    weight = root * jnp.broadcast_to(scale, (128, CORE)).T
    weight_column[:CORE, :] = weight
    weight_column[CORE:, :] = root_column[CORE:, :]
    across = root_row[0:1, :CORE] * scale
    weight_row[0:1, :CORE] = across
    weight_row[0:1, CORE:] = root_row[0:1, CORE:]
    lifted = jnp.tile(weight, (1, CORE // 128)) * covariance
    basis[:CORE, :] = lifted
    first[:CORE, :CORE] = lifted.astype(BF16)
    block = lifted * across
    gram[:CORE, :CORE] = block.astype(BF16)
    pull = ratio_column[:CORE, :] - root * jnp.broadcast_to(mean, (128, CORE)).T
    pulls[:CORE, :] = pull
    first[:CORE, CORE:] = pull.astype(BF16)
    sums[0:8, :] = jnp.broadcast_to(squared(block), (8, 128))
    sums[8:16, :] = jnp.broadcast_to(corners(block), (8, 128))


def add_rim(
    rims, top, earlier, ratio_column,
    window, gram, basis, first, pulls, weight_column, weight_row,
):
    span = slice(top, top + RIM)
    live = (lax.broadcasted_iota(I32, (RIM, ROWS), 1) & (PADDED - 1)) < HELD
    tile = rims[...].astype(F32)
    mean = jnp.sum(tile, axis=1, keepdims=True) / MEMBERS
    weight = weight_column[span, :]
    seen = jnp.where(weight[:, 0:1] > 0.0, 1.0, 0.0)
    strip = jnp.where(live, (tile - mean) * seen, 0.0).astype(BF16)
    pull = ratio_column[span, :] - weight * mean
    pulls[span, :] = pull
    first[span, CORE:] = pull.astype(BF16)
    lifted = jnp.tile(weight, (1, CORE // 128)) * mm(strip, window[:, :CORE])
    basis[span, :] = lifted
    first[span, :CORE] = lifted.astype(BF16)
    block = lifted * weight_row[0:1, :CORE]
    gram[span, :CORE] = block.astype(BF16)
    gram[:CORE, span] = block.astype(BF16).T
    squares = 2.0 * squared(block)
    weight = weight[:, 0:1]
    if earlier is not None:
        block = weight * mm_nt(strip, earlier[...]) * weight_row[0:1, CORE : CORE + RIM]
        gram[span, CORE : CORE + RIM] = block.astype(BF16)
        gram[CORE : CORE + RIM, span] = block.astype(BF16).T
        squares += 2.0 * squared(block)
    block = weight * mm_nt(strip, strip) * weight_row[0:1, span]
    gram[span, span] = block.astype(BF16)
    return strip, squares + squared(block), corners(block)


def before_kernel(
    before, own_sums, ratio_column,
    _window, _gram, _basis, _first, _pulls, _weight_column, _weight_row,
    window, gram, basis, first, pulls, weight_column, weight_row, strip, sums,
):
    added, squares, trace = add_rim(
        before, CORE, None, ratio_column,
        window, gram, basis, first, pulls, weight_column, weight_row,
    )
    strip[...] = added
    window[:, CORE : CORE + RIM] = added.T
    sums[0:8, :] = own_sums[0:8, :] + squares
    sums[8:16, :] = own_sums[8:16, :] + trace


def analyse_kernel(
    after, strip, state_mean, sums, ratio_column,
    _window, _gram, _basis, _first, _pulls, _weight_column, _weight_row,
    window, gram, basis, first, pulls, weight_column, weight_row, out, second, third, fourth,
):
    added, squares, trace = add_rim(
        after, CORE + RIM, strip, ratio_column,
        window, gram, basis, first, pulls, weight_column, weight_row,
    )
    squares += sums[0:1, 0:1]
    trace += sums[8:9, 0:1]
    draw = F32(MEMBERS - 1)
    inverse = 1.0 / (draw + 2.0 * squares / (draw + trace))

    a = draw * inverse
    r = 1.5 - 0.5 * a
    s = 1.5 - 0.5 * a * r * r
    halves = ((slice(0, 256), slice(0, 256)), (slice(256, CORE), slice(0, 128)))
    last = slice(CORE, CORE + 128)

    def product(source, h):
        return mm(gram[...], source[:, h * 256 : (h + 1) * 256])

    def one(h, p):
        wide, part = halves[h]
        v = (0.25 * inverse * inverse) * p[:, part] - (r * inverse) * basis[:, wide]
        second[:, wide] = v.astype(BF16)
        if h:
            second[:, last] = (r * pulls[...] - (0.5 * inverse) * p[:, 128:]).astype(BF16)

    def two(h, p):
        wide, part = halves[h]
        v = (-0.5 * a) * second[:, wide].astype(F32) - (0.5 * inverse) * p[:, part]
        v -= (0.5 * r * r * inverse) * basis[:, wide]
        third[:, wide] = v.astype(BF16)
        if h:
            x = r * second[:, last].astype(F32) - (0.5 * inverse) * p[:, 128:]
            third[:, last] = x.astype(BF16)

    def three(h, p):
        wide, part = halves[h]
        v = r * third[:, wide].astype(F32) - (0.5 * inverse) * p[:, part]
        v -= (0.5 * s * inverse) * basis[:, wide]
        fourth[:, wide] = v.astype(BF16)
        first[:, wide] = (jnp.tile(weight_column[...], (1, v.shape[1] // 128)) * v).astype(BF16)
        if h:
            x = (-0.5 * a) * third[:, last].astype(F32) - (0.5 * inverse) * p[:, 128:]
            fourth[:, last] = (1.5 * pulls[...] + x).astype(BF16)

    chain = (first, second, third, fourth)
    late = product(first, 1)
    waiting = [product(first, 0), late]
    window[:, CORE + RIM :] = added.T
    for k, finish in enumerate((one, two, three)):
        for h in (1, 0):
            finish(h, waiting[h])
            waiting[h] = product(chain[k + 1], h)
    x = r * fourth[:, last].astype(F32) - (0.5 * inverse) * waiting[1][:, 128:]
    x *= inverse
    shift = []
    for h, (wide, part) in enumerate(halves):
        for t in range(part.start, part.stop, 128):
            both = (r * s) * basis[:, h * 256 + t : h * 256 + t + 128] + waiting[h][:, t : t + 128]
            shift.append(jnp.sum(x * both, axis=0, keepdims=True))
    scale = state_mean[1:2, :]
    base = state_mean[0:1, :] + scale * jnp.concatenate(shift, axis=1)
    gain = jnp.sqrt(a) * scale
    for t in range(0, ROWS, TILE):
        rows = slice(t, t + TILE)
        moved = mm(window[rows, :], first[:, :CORE])
        moved += r * s * window[rows, :CORE].astype(F32)
        out[rows, :] = (base + gain * moved).astype(BF16)


def call(
    kernel, name, in_specs, out_shape, out_specs=None, scratch_shapes=(), flops=0, aliases=None
):
    return pl.pallas_call(
        kernel,
        in_specs=in_specs,
        out_specs=out_specs or jax.tree.map(lambda _: vmem(), out_shape),
        out_shape=out_shape,
        scratch_shapes=list(scratch_shapes),
        input_output_aliases=aliases or {},
        compiler_params=params(),
        cost_estimate=pl.CostEstimate(flops=flops, bytes_accessed=1 << 20, transcendentals=0),
        name=name,
    )


def enter(states):
    return call(
        entry_kernel, "entry", [vmem()], shape(GROUP, PADDED, CORE), flops=8 * 256 * 256 * CORE
    )(states)


def leave(analysed):
    return call(
        exit_kernel, "exit", [vmem()], shape(HELD, GROUP, CORE), hbm(),
        [pltpu.VMEM((HELD, GROUP, CORE), BF16), pltpu.SemaphoreType.DMA((4,))],
        8 * 256 * 256 * CORE,
    )(analysed)


def prepare(hosted, tally, taper, location, datum, error_spread, band):
    return call(
        prepare_kernel, "prepare", [smem()] * 3 + [vmem()] * 4,
        [shape(SPAN, 128, dtype=F32), shape(SPAN, 128, dtype=F32), shape(8, SPAN, dtype=F32),
         shape(2 * RIM, CORE)],
        flops=4 * SPAN * OBS,
    )(hosted, tally, taper, location, datum, error_spread, band)


def extract(states, pick):
    return call(
        extract_kernel, "extract", [vmem()] * 2, [shape(RIM, ROWS), shape(RIM, ROWS)],
        flops=4 * RIM * CORE * ROWS,
    )(states, pick)


def growing():
    return [
        shape(ROWS, SPAN), shape(SPAN, SPAN), shape(SPAN, CORE, dtype=F32),
        shape(SPAN, CORE + 128), shape(SPAN, 128, dtype=F32),
        shape(SPAN, 128, dtype=F32), shape(8, SPAN, dtype=F32),
    ]


def own_part(states, prepared):
    *grown, state_mean, sums = call(
        own_kernel, "own_part", [vmem()] * 4,
        growing() + [shape(8, CORE, dtype=F32), shape(16, 128, dtype=F32)],
        flops=2 * ROWS * CORE * CORE,
    )(states, *prepared)
    return grown, state_mean, sums


def before_part(before, grown, sums, prepared):
    *grown, strip, sums = call(
        before_kernel, "before_part", [vmem()] * 10,
        growing() + [shape(RIM, ROWS), shape(16, 128, dtype=F32)],
        flops=2 * ROWS * RIM * (CORE + RIM), aliases={3 + k: k for k in range(7)},
    )(before, sums, prepared[1], *grown)
    return grown, strip, sums


def analyse(after, grown, strip, state_mean, sums, prepared):
    chain = pltpu.VMEM((SPAN, CORE + 128), BF16)
    return call(
        analyse_kernel, "analyse", [vmem()] * 12, growing() + [shape(ROWS, CORE)],
        scratch_shapes=[chain, chain, chain],
        flops=8 * SPAN * SPAN * CORE, aliases={5 + k: k for k in range(7)},
    )(after, strip, state_mean, sums, prepared[1], *grown)[-1]


def local(
    background_fields,
    measured_location,
    measured_datum,
    measured_error_spread,
    measured_distance_band,
    measured_tally,
    taper_weights,
):
    axes = ("member", "patch")
    groups = lax.axis_size("patch")
    sent = enter(jnp.transpose(background_fields, (1, 0, 2)))
    received = lax.all_to_all(sent, "member", split_axis=0, concat_axis=0, tiled=True)
    *prepared, pick = prepare(
        jnp.asarray(HOSTED), measured_tally, taper_weights, measured_location, measured_datum,
        measured_error_spread, measured_distance_band,
    )
    states = received.reshape(ROWS, CORE)
    rightward, leftward = extract(states, pick)
    owners = [CYCLES[g % 2][p] * groups + g for g in range(groups) for p in range(GROUP)]
    up = list(zip(owners, owners[1:] + owners[:1]))
    down = [(j, i) for i, j in up]
    before = lax.ppermute(rightward, axes, up)
    after = lax.ppermute(leftward, axes, down)
    grown, state_mean, sums = own_part(states, prepared)
    grown, strip, sums = before_part(before, grown, sums, prepared)
    analysed = analyse(after, grown, strip, state_mean, sums, prepared)
    analysed = analysed.reshape(GROUP, PADDED, CORE)
    returned = lax.all_to_all(analysed, "member", split_axis=0, concat_axis=0, tiled=True)
    return jnp.transpose(leave(returned), (1, 0, 2))


def solution(mesh):
    placed = (
        P("patch", "member", None),
        P("patch", None),
        P("patch", None),
        P("patch", None),
        P("patch", None),
        P("patch"),
        P(),
    )
    return jax.shard_map(
        local, mesh=mesh, in_specs=placed, out_specs=P("patch", "member", None), check_vma=False
    )
```
